256 devices in a mesh: ta: 8 (over y, core), ha: 4 (over x), wa: 8 (over z).
Axes of the slice: x: 4, y: 4, z: 8, core: 2. Of those that a mesh axis runs over, the one named last changes fastest.
Arguments:
- latent: bfloat16 [32, 16, 64, 512], P('ta', 'ha', 'wa'), may hold values from -6 to 6
- cotangent: bfloat16 [32, 32, 128, 512], P('ta', 'ha', 'wa'), may hold values from -6 to 6
- conv_bias: float32 [512], replicated, may hold values from -3 to 3
- conv_weight: bfloat16 [3, 3, 3, 512, 512], P(None, None, None, ('ha', 'wa')), may hold values from -0.0546875 to 0.0546875
- up_weight: bfloat16 [3, 3, 512, 512], P(None, None, ('ha', 'wa')), may hold values from -0.09375 to 0.09375
Outputs:
- latent_grad: bfloat16 [32, 16, 64, 512], P('ta', 'ha', 'wa')
The draws below stay inside these ranges and needn't reach their ends.
All inputs are finite; a program needn't handle non-finite values.
Results may differ from the reference program's by a relative error of at most 0.0049.
Values may be sent and summed in bfloat16 or wider, within the bound.
No kernel may reach another device: no remote copies, remote signals or barrier semaphores. Data moves between devices by JAX's collectives and lax.ppermute only.
A program may use at most 128 MiB of HBM per device.

```python
import jax
import jax.numpy as jnp
from jax import lax

CH = 512
NT = 32
NH = 16
NW = 64


def block_scale(key, dims, shards, low, largest):
    gain = 1.0
    for dim, blocks in shards:
        draws = jax.random.uniform(jax.random.fold_in(jax.random.fold_in(key, 6), dim), (blocks,), jnp.float32, low / len(shards), largest / len(shards))
        gain = gain * jnp.repeat(jnp.exp(draws), dims[dim] // blocks).reshape((-1,) + (1,) * (len(dims) - 1 - dim))
    return gain


def normal_values(key, extent, deviation, reach, pieces=(), kind=jnp.bfloat16):
    level = block_scale(key, extent, pieces, -0.22, 0.18) if pieces else 1.0
    values = jax.random.normal(key, extent, jnp.float32) * deviation * level
    return jnp.minimum(jnp.maximum(values, -reach), reach).astype(kind)


def setup_inputs(seed: int = 0) -> dict:
    key_of = jax.random.split(jax.random.key(seed), 6)
    return {
        "latent": normal_values(key_of[0], (NT, NH, NW, CH), 1.0, 6.0, ((0, 8), (1, 4), (2, 8))),
        "cotangent": normal_values(key_of[1], (NT, 2 * NH, 2 * NW, CH), 1.0, 6.0, ((0, 8), (1, 4), (2, 8))),
        "conv_bias": normal_values(key_of[2], (CH,), 0.5, 3.0, (), jnp.float32),
        "conv_weight": normal_values(key_of[3], (3, 3, 3, CH, CH), (27 * CH) ** -0.5, 0.0546875, ((3, 32),)),
        "up_weight": normal_values(key_of[4], (3, 3, CH, CH), (9 * CH) ** -0.5, 0.09375, ((2, 32),)),
    }


def conv_taps(padded, weight, backward):
    depth = weight.shape[0]
    frames = padded.shape[0] - depth + 1
    row_count = padded.shape[1] - 2
    col_count = padded.shape[2] - 2
    out_chan = weight.shape[3] if backward else weight.shape[4]
    summed = jnp.zeros((frames * row_count * col_count, out_chan), jnp.float32)
    for tap_t in range(depth):
        for tap_h in range(3):
            for tap_w in range(3):
                if backward:
                    off_t, off_h, off_w = depth - 1 - tap_t, 2 - tap_h, 2 - tap_w
                else:
                    off_t, off_h, off_w = tap_t, tap_h, tap_w
                window = padded[off_t:off_t + frames, off_h:off_h + row_count, off_w:off_w + col_count]
                window = window.reshape(-1, padded.shape[3])
                kernel = weight[tap_t, tap_h, tap_w]
                if backward:
                    summed = summed + lax.dot_general(window, kernel, (((1,), (1,)), ((), ())), preferred_element_type=jnp.float32)
                else:
                    summed = summed + jnp.dot(window, kernel, preferred_element_type=jnp.float32)
    return summed.reshape(frames, row_count, col_count, out_chan)


def reference(latent, cotangent, conv_bias, conv_weight, up_weight):
    n_frames, n_rows, n_cols, chans = latent.shape
    padded_in = jnp.concatenate([latent[:1], latent[:1], latent], axis=0)
    padded_in = jnp.pad(padded_in, ((0, 0), (1, 1), (1, 1), (0, 0)))
    pre_act = conv_taps(padded_in, conv_weight, False) + conv_bias
    cot_pad = jnp.pad(cotangent, ((0, 0), (1, 1), (1, 1), (0, 0)))
    grad_up = conv_taps(cot_pad, up_weight[None], True)
    grad_act = grad_up.reshape(n_frames, n_rows, 2, n_cols, 2, chans).sum(axis=(2, 4))
    sigmoid_h = jax.nn.sigmoid(pre_act)
    grad_pre = (grad_act * sigmoid_h * (1.0 + pre_act * (1.0 - sigmoid_h))).astype(jnp.bfloat16)
    grad_zpad = jnp.pad(grad_pre, ((2, 2), (1, 1), (1, 1), (0, 0)))
    full_grad = conv_taps(grad_zpad, conv_weight, True)
    result = full_grad[2:]
    result = result.at[0].add(full_grad[0] + full_grad[1])
    return result.astype(jnp.bfloat16)
```

```python
import functools

import jax
import jax.numpy as jnp
from jax import lax
from jax.experimental import pallas as pl
from jax.experimental.pallas import tpu as pltpu
from jax.sharding import PartitionSpec as P

F32, BF16 = jnp.float32, jnp.bfloat16
LANES = 128
VMEM_LIMIT = 48 * 1024 * 1024


def roll_rows(x, shift):
    return pltpu.roll(x, shift, x.ndim - 2)


def row_in_block(shape):
    return lax.broadcasted_iota(jnp.int32, shape, len(shape) - 2) % 4


def from_above(x):
    prev = jnp.concatenate([jnp.zeros_like(x[:, :1]), x[:, :-1]], axis=1)
    n = x.shape[2]
    return jnp.where(row_in_block(x.shape) == 0, roll_rows(prev, n - 3), roll_rows(x, 1))


def from_below(x):
    later = jnp.concatenate([x[:, 1:], jnp.zeros_like(x[:, :1])], axis=1)
    n = x.shape[2]
    return jnp.where(row_in_block(x.shape) == 3, roll_rows(later, 3), roll_rows(x, n - 1))


def weight_copies(own_ref, other_ref, groups, first, w_ref, sem):
    n_wa, n_ha, half, shard, _ = own_ref.shape
    core = lax.rem(lax.axis_index("ta"), 2)
    spans = [
        (max(first, part * half), min(first + groups, (part + 1) * half), part) for part in (0, 1)
    ]
    spans = [s for s in spans if s[0] < s[1]]

    def each(action):
        for index, (lo, hi, part) in enumerate(spans):
            for holder, src in ((part, own_ref), (1 - part, other_ref)):

                @pl.when(core == holder)
                def _(lo=lo, hi=hi, part=part, src=src, index=index):
                    for wa in range(n_wa):
                        for ha in range(n_ha):
                            row = ha * n_wa * shard + wa * shard
                            copy = pltpu.make_async_copy(
                                src.at[wa, ha, pl.ds(lo - part * half, hi - lo)],
                                w_ref.at[pl.ds(lo - first, hi - lo), pl.ds(row, shard)],
                                sem.at[index, wa, ha],
                            )
                            getattr(copy, action)()

    return functools.partial(each, "start"), functools.partial(each, "wait")


def up_kernel(cot_ref, own_ref, other_ref, out_ref, w_ref, rows_ref, sem):
    start, wait = weight_copies(own_ref, other_ref, 3, 9, w_ref, sem)
    start()
    n_ha = cot_ref.shape[0]
    for par in range(2):
        cot = jnp.stack([cot_ref[x, par] for x in range(n_ha)], axis=1).astype(F32)
        even, odd = cot[:, :, 0], cot[:, :, 1]
        rows_ref[par, :, :, :, 0:LANES] = odd + from_below(even)
        rows_ref[par, :, :, :, LANES : 2 * LANES] = even + odd
        rows_ref[par, :, :, :, 2 * LANES : 3 * LANES] = even + from_above(odd)
    wait()
    total = None
    for b in range(3):
        box = None
        for e in (1 - b, 2 - b):
            par, off = (e + 1) % 2, (e + 1) // 2
            part = rows_ref[par, off : off + 8]
            box = part if box is None else box + part
        box = box.reshape(-1, 3 * LANES)
        high = box.astype(BF16)
        low = (box - high.astype(F32)).astype(BF16)
        for piece in (high, low):
            term = lax.dot_general(
                piece, w_ref[b], (((1,), (1,)), ((), ())), preferred_element_type=F32
            )
            total = term if total is None else total + term
    for x in range(n_ha):
        out_ref[x] = total[:, x * LANES : (x + 1) * LANES].astype(BF16)


def fwd_kernel(lat_ref, own_ref, other_ref, bias_ref, act_ref, out_ref, w_ref, win_ref, sem):
    start, wait = weight_copies(own_ref, other_ref, 9, 0, w_ref, sem)
    start()
    n_ha = lat_ref.shape[0]
    for x in range(n_ha):
        for pair in range(5):
            two = lat_ref[x, pair * 48 : pair * 48 + 48, :].astype(F32)
            for one in range(2):
                for k in range(3):
                    lo = one * 24 + 4 * k
                    win_ref[k, 2 * pair + one, x] = two[lo : lo + 16].astype(BF16)
    wait()
    total = None
    for k in range(3):
        for b in range(3):
            window = win_ref[k, b : b + 8].reshape(-1, win_ref.shape[-1])
            term = jnp.dot(window, w_ref[3 * k + b], preferred_element_type=F32)
            total = term if total is None else total + term
    total = total.reshape(8, n_ha, 16, 3 * LANES)
    pre = (
        from_above(total[..., :LANES])
        + total[..., LANES : 2 * LANES]
        + from_below(total[..., 2 * LANES :])
        + bias_ref[...].reshape(1, 1, 1, LANES)
    )
    grad = act_ref[0].astype(F32)
    for x in range(1, n_ha):
        grad = grad + act_ref[x].astype(F32)
    grad = grad.reshape(pre.shape)
    sig = 1.0 / (1.0 + jnp.exp(-pre))
    out_ref[...] = (grad * sig * (1.0 + pre * (1.0 - sig))).astype(BF16)


def bwd_kernel(g_ref, later_ref, left_ref, right_ref, own_ref, other_ref, out_ref, w_ref, win_ref, sem):
    start, wait = weight_copies(own_ref, other_ref, 9, 0, w_ref, sem)
    start()
    n_ha = g_ref.shape[1]
    at_start = (lax.axis_index("ta") == 0).astype(F32)
    grad = jnp.concatenate([g_ref[...].astype(F32), later_ref[...].astype(F32)], axis=2)
    grad = jnp.concatenate(
        [left_ref[...].astype(F32)[None], grad, right_ref[...].astype(F32)[None]], axis=0
    )
    zero, one, two = grad[:, :, 0:4], grad[:, :, 4:8], grad[:, :, 8:12]
    windows = [
        grad[:, :, 0:16],
        jnp.concatenate([one + at_start * zero, grad[:, :, 8:20]], axis=2),
        jnp.concatenate([two + at_start * (zero + one), grad[:, :, 12:24]], axis=2),
    ]
    for shift in range(3):
        x = windows[shift]
        win_ref[shift, :, :, :, 0:LANES] = from_below(x).astype(BF16)
        win_ref[shift, :, :, :, LANES : 2 * LANES] = x.astype(BF16)
        win_ref[shift, :, :, :, 2 * LANES : 3 * LANES] = from_above(x).astype(BF16)
    wait()
    total = None
    for k in range(3):
        for b in range(3):
            window = win_ref[2 - k, 2 - b : 10 - b].reshape(-1, 3 * LANES)
            term = lax.dot_general(
                window, w_ref[3 * k + b], (((1,), (1,)), ((), ())), preferred_element_type=F32
            )
            total = term if total is None else total + term
    total = total.astype(BF16).reshape(8, n_ha, 16, -1)
    for x in range(n_ha):
        out_ref[x] = total[:, x]


def call(kernel, out_shape, specs, scratch):
    return pl.pallas_call(
        kernel,
        out_shape=out_shape,
        in_specs=specs,
        out_specs=pl.BlockSpec(memory_space=pltpu.VMEM),
        scratch_shapes=scratch,
        compiler_params=pltpu.CompilerParams(vmem_limit_bytes=VMEM_LIMIT),
    )


def shifted(x, axis, step):
    n = lax.axis_size(axis)
    return lax.ppermute(x, axis, [(i, i + step) for i in range(n) if 0 <= i + step < n])


def on_device(latent, cotangent, conv_bias, conv_weight, up_weight):
    frames, rows, cols, chans = latent.shape
    n_ta, n_ha, n_wa = (lax.axis_size(a) for a in ("ta", "ha", "wa"))
    ta, ha = lax.axis_index("ta"), lax.axis_index("ha")
    shard = conv_weight.shape[3]
    core = lax.rem(ta, 2)

    conv_g = conv_weight.reshape(3, 3, 3, shard, n_ha, LANES).transpose(4, 0, 2, 3, 1, 5)
    up_g = up_weight.reshape(3, 3, shard, n_ha, LANES).transpose(3, 1, 2, 0, 4)
    groups = jnp.concatenate(
        [conv_g.reshape(n_ha, 9, shard, 3 * LANES), up_g.reshape(n_ha, 3, shard, 3 * LANES)], axis=1
    )
    groups = lax.dynamic_slice_in_dim(groups, 6 * core, 6, axis=1)
    groups = lax.all_to_all(groups, "ha", 0, 0)
    w_own = lax.all_gather(groups, "wa", axis=0)
    w_other = lax.ppermute(w_own, "ta", [(i, i ^ 1) for i in range(n_ta)])

    past = shifted(latent[frames - 2 :], "ta", 1)
    past = jnp.where(ta == 0, jnp.broadcast_to(latent[:1], past.shape), past)
    ext = jnp.concatenate([past, latent], axis=0)

    def edge(col_l, col_c):
        return jnp.concatenate(
            [ext[:, :, col_l].reshape(-1, chans), cotangent[:, :, col_c].reshape(-1, chans)], axis=0
        )

    split = (frames + 2) * rows
    left = shifted(edge(cols - 1, 2 * cols - 1), "wa", 1)
    right = shifted(edge(0, 0), "wa", -1)

    def lat_col(x):
        return x[:split].reshape(frames + 2, rows, 1, chans)

    def cot_col(x):
        return x[split:].reshape(frames, 2 * rows, 1, chans)

    lat = jnp.concatenate([lat_col(left), ext, lat_col(right)], axis=2)
    lat = lat.transpose(2, 0, 1, 3).reshape((cols + 2) * split, chans)
    lat = lax.all_gather(lat, "ha", axis=0)
    cot = jnp.concatenate([cot_col(left), cotangent, cot_col(right)], axis=2)
    cot = cot.reshape(frames, rows, 2, cols + 1, 2, n_ha, LANES).transpose(5, 4, 3, 2, 0, 1, 6)
    cot = cot.reshape(n_ha, 2, cols + 1, 2, frames * rows, LANES)
    cot = lax.all_to_all(cot, "ha", 0, 0)

    vmem, anywhere = pl.BlockSpec(memory_space=pltpu.VMEM), pl.BlockSpec(memory_space=pl.ANY)
    points = cols * n_ha * frames * rows
    sem = pltpu.SemaphoreType.DMA((2, n_wa, n_ha))
    w_conv = pltpu.VMEM((9, chans, 3 * LANES), BF16)

    act = call(
        up_kernel,
        jax.ShapeDtypeStruct((n_ha, points, LANES), BF16),
        [vmem, anywhere, anywhere],
        [
            pltpu.VMEM((3, chans, 3 * LANES), BF16),
            pltpu.VMEM((2, cols + 1, n_ha, frames * rows, 3 * LANES), F32),
            sem,
        ],
    )(cot, w_own, w_other)
    act = lax.all_to_all(act, "ha", 0, 0)

    bias = lax.dynamic_slice_in_dim(conv_bias, ha * LANES, LANES).reshape(1, LANES)
    grad = call(
        fwd_kernel,
        jax.ShapeDtypeStruct((cols, n_ha, frames * rows, LANES), BF16),
        [vmem, anywhere, anywhere, vmem, vmem],
        [w_conv, pltpu.VMEM((3, cols + 2, n_ha, frames * rows, chans), BF16), sem],
    )(lat, w_own, w_other, bias, act)

    later = shifted(grad[:, :, : 2 * rows], "ta", -1)
    g_left = shifted(jnp.concatenate([grad[cols - 1], later[cols - 1]], axis=1), "wa", 1)
    g_right = shifted(jnp.concatenate([grad[0], later[0]], axis=1), "wa", -1)

    out = call(
        bwd_kernel,
        jax.ShapeDtypeStruct((n_ha, cols, frames * rows, chans), BF16),
        [vmem, vmem, vmem, vmem, anywhere, anywhere],
        [w_conv, pltpu.VMEM((3, cols + 2, n_ha, frames * rows, 3 * LANES), BF16), sem],
    )(grad, later, g_left, g_right, w_own, w_other)
    out = lax.all_to_all(out, "ha", 0, 0)
    out = out.astype(F32).sum(axis=0).reshape(cols, frames, rows, chans)
    return out.transpose(1, 2, 0, 3).astype(BF16)


def solution(mesh):
    in_specs = (
        P("ta", "ha", "wa", None),
        P("ta", "ha", "wa", None),
        P(),
        P(None, None, None, ("ha", "wa"), None),
        P(None, None, ("ha", "wa"), None),
    )
    return jax.shard_map(
        on_device, mesh=mesh, in_specs=in_specs, out_specs=P("ta", "ha", "wa", None), check_vma=False
    )
```

```python
import functools

import jax
import jax.numpy as jnp
from jax import lax
from jax.experimental import pallas as pl
from jax.experimental.pallas import tpu as pltpu
from jax.sharding import PartitionSpec as P

F32, BF16 = jnp.float32, jnp.bfloat16
LANES = 128
VMEM_LIMIT = 48 * 1024 * 1024


def roll_rows(x, shift):
    return pltpu.roll(x, shift, x.ndim - 2)


def row_in_block(shape):
    return lax.broadcasted_iota(jnp.int32, shape, len(shape) - 2) % 4


def from_above(x):
    prev = jnp.concatenate([jnp.zeros_like(x[:, :1]), x[:, :-1]], axis=1)
    n = x.shape[2]
    return jnp.where(row_in_block(x.shape) == 0, roll_rows(prev, n - 3), roll_rows(x, 1))


def from_below(x):
    later = jnp.concatenate([x[:, 1:], jnp.zeros_like(x[:, :1])], axis=1)
    n = x.shape[2]
    return jnp.where(row_in_block(x.shape) == 3, roll_rows(later, 3), roll_rows(x, n - 1))


def weight_copies(own_ref, other_ref, groups, first, w_ref, sem):
    n_wa, n_ha, half, shard, _ = own_ref.shape
    core = lax.rem(lax.axis_index("ta"), 2)
    spans = [
        (max(first, part * half), min(first + groups, (part + 1) * half), part) for part in (0, 1)
    ]
    spans = [s for s in spans if s[0] < s[1]]

    def each(action):
        for index, (lo, hi, part) in enumerate(spans):
            for holder, src in ((part, own_ref), (1 - part, other_ref)):

                @pl.when(core == holder)
                def _(lo=lo, hi=hi, part=part, src=src, index=index):
                    for wa in range(n_wa):
                        for ha in range(n_ha):
                            row = ha * n_wa * shard + wa * shard
                            copy = pltpu.make_async_copy(
                                src.at[wa, ha, pl.ds(lo - part * half, hi - lo)],
                                w_ref.at[pl.ds(lo - first, hi - lo), pl.ds(row, shard)],
                                sem.at[index, wa, ha],
                            )
                            getattr(copy, action)()

    return functools.partial(each, "start"), functools.partial(each, "wait")


def up_kernel(cot_ref, own_ref, other_ref, out_ref, w_ref, rows_ref, sem):
    start, wait = weight_copies(own_ref, other_ref, 3, 9, w_ref, sem)
    start()
    n_ha = cot_ref.shape[0]
    for par in range(2):
        cot = jnp.stack([cot_ref[x, par] for x in range(n_ha)], axis=1).astype(F32)
        even, odd = cot[:, :, 0], cot[:, :, 1]
        rows_ref[par, :, :, :, 0:LANES] = odd + from_below(even)
        rows_ref[par, :, :, :, LANES : 2 * LANES] = even + odd
        rows_ref[par, :, :, :, 2 * LANES : 3 * LANES] = even + from_above(odd)
    wait()
    total = None
    for b in range(3):
        box = None
        for e in (1 - b, 2 - b):
            par, off = (e + 1) % 2, (e + 1) // 2
            part = rows_ref[par, off : off + 8]
            box = part if box is None else box + part
        box = box.reshape(-1, 3 * LANES)
        high = box.astype(BF16)
        low = (box - high.astype(F32)).astype(BF16)
        for piece in (high, low):
            term = lax.dot_general(
                piece, w_ref[b], (((1,), (1,)), ((), ())), preferred_element_type=F32
            )
            total = term if total is None else total + term
    for x in range(n_ha):
        out_ref[x] = total[:, x * LANES : (x + 1) * LANES].astype(BF16)


def fwd_kernel(lat_ref, own_ref, other_ref, bias_ref, out_ref, w_ref, win_ref, sem):
    start, wait = weight_copies(own_ref, other_ref, 9, 0, w_ref, sem)
    start()
    n_ha = lat_ref.shape[0]
    for x in range(n_ha):
        for pair in range(5):
            two = lat_ref[x, pair * 48 : pair * 48 + 48, :].astype(F32)
            for one in range(2):
                for k in range(3):
                    lo = one * 24 + 4 * k
                    win_ref[k, 2 * pair + one, x] = two[lo : lo + 16].astype(BF16)
    wait()
    total = None
    for k in range(3):
        for b in range(3):
            window = win_ref[k, b : b + 8].reshape(-1, win_ref.shape[-1])
            term = jnp.dot(window, w_ref[3 * k + b], preferred_element_type=F32)
            total = term if total is None else total + term
    total = total.reshape(8, n_ha, 16, 3 * LANES)
    pre = (
        from_above(total[..., :LANES])
        + total[..., LANES : 2 * LANES]
        + from_below(total[..., 2 * LANES :])
        + bias_ref[...].reshape(1, 1, 1, LANES)
    )
    sig = 1.0 / (1.0 + jnp.exp(-pre))
    out_ref[...] = sig * (1.0 + pre * (1.0 - sig))


def gate_kernel(slope_ref, act_ref, out_ref):
    grad = act_ref[0].astype(F32)
    for x in range(1, act_ref.shape[0]):
        grad = grad + act_ref[x].astype(F32)
    out_ref[...] = (grad.reshape(slope_ref.shape) * slope_ref[...]).astype(BF16)


def bwd_kernel(g_ref, later_ref, left_ref, right_ref, own_ref, other_ref, out_ref, w_ref, win_ref, sem):
    start, wait = weight_copies(own_ref, other_ref, 9, 0, w_ref, sem)
    start()
    n_ha = g_ref.shape[1]
    at_start = (lax.axis_index("ta") == 0).astype(F32)
    grad = jnp.concatenate([g_ref[...].astype(F32), later_ref[...].astype(F32)], axis=2)
    grad = jnp.concatenate(
        [left_ref[...].astype(F32)[None], grad, right_ref[...].astype(F32)[None]], axis=0
    )
    zero, one, two = grad[:, :, 0:4], grad[:, :, 4:8], grad[:, :, 8:12]
    windows = [
        grad[:, :, 0:16],
        jnp.concatenate([one + at_start * zero, grad[:, :, 8:20]], axis=2),
        jnp.concatenate([two + at_start * (zero + one), grad[:, :, 12:24]], axis=2),
    ]
    for shift in range(3):
        x = windows[shift]
        win_ref[shift, :, :, :, 0:LANES] = from_below(x).astype(BF16)
        win_ref[shift, :, :, :, LANES : 2 * LANES] = x.astype(BF16)
        win_ref[shift, :, :, :, 2 * LANES : 3 * LANES] = from_above(x).astype(BF16)
    wait()
    total = None
    for k in range(3):
        for b in range(3):
            window = win_ref[2 - k, 2 - b : 10 - b].reshape(-1, 3 * LANES)
            term = lax.dot_general(
                window, w_ref[3 * k + b], (((1,), (1,)), ((), ())), preferred_element_type=F32
            )
            total = term if total is None else total + term
    total = total.astype(BF16).reshape(8, n_ha, 16, -1)
    for x in range(n_ha):
        out_ref[x] = total[:, x]


def call(kernel, out_shape, specs, scratch, cost=None):
    return pl.pallas_call(
        kernel,
        out_shape=out_shape,
        in_specs=specs,
        out_specs=pl.BlockSpec(memory_space=pltpu.VMEM),
        scratch_shapes=scratch,
        cost_estimate=cost,
        compiler_params=pltpu.CompilerParams(vmem_limit_bytes=VMEM_LIMIT),
    )


def shifted(x, axis, step):
    n = lax.axis_size(axis)
    return lax.ppermute(x, axis, [(i, i + step) for i in range(n) if 0 <= i + step < n])


def on_device(latent, cotangent, conv_bias, conv_weight, up_weight):
    frames, rows, cols, chans = latent.shape
    n_ta, n_ha, n_wa = (lax.axis_size(a) for a in ("ta", "ha", "wa"))
    ta, ha = lax.axis_index("ta"), lax.axis_index("ha")
    shard = conv_weight.shape[3]
    core = lax.rem(ta, 2)

    conv_g = conv_weight.reshape(3, 3, 3, shard, n_ha, LANES).transpose(4, 0, 2, 3, 1, 5)
    up_g = up_weight.reshape(3, 3, shard, n_ha, LANES).transpose(3, 1, 2, 0, 4)
    groups = jnp.concatenate(
        [conv_g.reshape(n_ha, 9, shard, 3 * LANES), up_g.reshape(n_ha, 3, shard, 3 * LANES)], axis=1
    )
    groups = lax.dynamic_slice_in_dim(groups, 6 * core, 6, axis=1)
    groups = lax.all_to_all(groups, "ha", 0, 0)
    w_own = lax.all_gather(groups, "wa", axis=0)

    past = shifted(latent[frames - 2 :], "ta", 1)
    past = jnp.where(ta == 0, jnp.broadcast_to(latent[:1], past.shape), past)
    ext = jnp.concatenate([past, latent], axis=0)

    def edge(col_l, col_c):
        return jnp.concatenate(
            [ext[:, :, col_l].reshape(-1, chans), cotangent[:, :, col_c].reshape(-1, chans)], axis=0
        )

    split = (frames + 2) * rows
    left = shifted(edge(cols - 1, 2 * cols - 1), "wa", 1)
    right = shifted(edge(0, 0), "wa", -1)

    def lat_col(x):
        return x[:split].reshape(frames + 2, rows, 1, chans)

    def cot_col(x):
        return x[split:].reshape(frames, 2 * rows, 1, chans)

    lat = jnp.concatenate([lat_col(left), ext, lat_col(right)], axis=2)
    lat = lat.transpose(2, 0, 1, 3).reshape((cols + 2) * split, chans)
    lat = lax.all_gather(lat, "ha", axis=0)
    cot = jnp.concatenate([cot_col(left), cotangent, cot_col(right)], axis=2)
    cot = cot.reshape(frames, rows, 2, cols + 1, 2, n_ha, LANES).transpose(5, 4, 3, 2, 0, 1, 6)
    cot = cot.reshape(n_ha, 2, cols + 1, 2, frames * rows, LANES)
    cot = lax.all_to_all(cot, "ha", 0, 0)

    w_own, lat, cot = lax.optimization_barrier((w_own, lat, cot))
    w_other = lax.ppermute(w_own, "ta", [(i, i ^ 1) for i in range(n_ta)])

    vmem, anywhere = pl.BlockSpec(memory_space=pltpu.VMEM), pl.BlockSpec(memory_space=pl.ANY)
    points = cols * n_ha * frames * rows
    sem = pltpu.SemaphoreType.DMA((2, n_wa, n_ha))
    w_conv = pltpu.VMEM((9, chans, 3 * LANES), BF16)

    act = call(
        up_kernel,
        jax.ShapeDtypeStruct((n_ha, points, LANES), BF16),
        [vmem, anywhere, anywhere],
        [
            pltpu.VMEM((3, chans, 3 * LANES), BF16),
            pltpu.VMEM((2, cols + 1, n_ha, frames * rows, 3 * LANES), F32),
            sem,
        ],
    )(cot, w_own, w_other)
    act = lax.all_to_all(act, "ha", 0, 0)

    bias = lax.dynamic_slice_in_dim(conv_bias, ha * LANES, LANES).reshape(1, LANES)
    slope = call(
        fwd_kernel,
        jax.ShapeDtypeStruct((cols, n_ha, frames * rows, LANES), F32),
        [vmem, anywhere, anywhere, vmem],
        [w_conv, pltpu.VMEM((3, cols + 2, n_ha, frames * rows, chans), BF16), sem],
        pl.CostEstimate(flops=3 * 9 * 2 * points * LANES * chans, bytes_accessed=5 << 20, transcendentals=0),
    )(lat, w_own, w_other, bias)
    grad = call(
        gate_kernel, jax.ShapeDtypeStruct((cols, n_ha, frames * rows, LANES), BF16), [vmem, vmem], []
    )(slope, act)

    later = shifted(grad[:, :, : 2 * rows], "ta", -1)
    g_left = shifted(jnp.concatenate([grad[cols - 1], later[cols - 1]], axis=1), "wa", 1)
    g_right = shifted(jnp.concatenate([grad[0], later[0]], axis=1), "wa", -1)

    out = call(
        bwd_kernel,
        jax.ShapeDtypeStruct((n_ha, cols, frames * rows, chans), BF16),
        [vmem, vmem, vmem, vmem, anywhere, anywhere],
        [w_conv, pltpu.VMEM((3, cols + 2, n_ha, frames * rows, 3 * LANES), BF16), sem],
    )(grad, later, g_left, g_right, w_own, w_other)
    out = lax.all_to_all(out, "ha", 0, 0)
    out = out.astype(F32).sum(axis=0).reshape(cols, frames, rows, chans)
    return out.transpose(1, 2, 0, 3).astype(BF16)


def solution(mesh):
    in_specs = (
        P("ta", "ha", "wa", None),
        P("ta", "ha", "wa", None),
        P(),
        P(None, None, None, ("ha", "wa"), None),
        P(None, None, ("ha", "wa"), None),
    )
    return jax.shard_map(
        on_device, mesh=mesh, in_specs=in_specs, out_specs=P("ta", "ha", "wa", None), check_vma=False
    )
```

```python
import functools

import jax
import jax.numpy as jnp
from jax import lax
from jax.experimental import pallas as pl
from jax.experimental.pallas import tpu as pltpu
from jax.sharding import PartitionSpec as P

F32, BF16 = jnp.float32, jnp.bfloat16
LANES = 128
VMEM_LIMIT = 24 * 1024 * 1024


def roll_rows(x, shift):
    return pltpu.roll(x, shift, x.ndim - 2)


def row_in_block(shape):
    return lax.broadcasted_iota(jnp.int32, shape, len(shape) - 2) % 4


def from_above(x):
    prev = jnp.concatenate([jnp.zeros_like(x[:, :1]), x[:, :-1]], axis=1)
    n = x.shape[2]
    return jnp.where(row_in_block(x.shape) == 0, roll_rows(prev, n - 3), roll_rows(x, 1))


def from_below(x):
    later = jnp.concatenate([x[:, 1:], jnp.zeros_like(x[:, :1])], axis=1)
    n = x.shape[2]
    return jnp.where(row_in_block(x.shape) == 3, roll_rows(later, 3), roll_rows(x, n - 1))


def weight_copies(whole, refs, lo, first, groups, to, w_ref, sem, base=0):
    core = lax.rem(lax.axis_index("ta"), 2)
    wa = lax.axis_index("wa")
    way = 1 - 2 * core
    rounds = len(refs) // 2 + 1
    n_wa, (n_ha, _, shard, _) = 2 * rounds, whole[0].shape
    half = n_ha // 2
    copies = []

    def copy(ref, at, begin, ha, place):
        row = pl.multiple_of((ha * n_wa + place) * shard, shard)
        copies.append(
            pltpu.make_async_copy(
                ref.at[at, pl.ds(begin, groups)],
                w_ref.at[pl.ds(to, groups), pl.ds(row, shard)],
                sem.at[base + len(copies)],
            )
        )

    def behind(r):
        return lax.rem(wa + n_wa + way * r, n_wa)

    for at in range(n_ha):
        copy(whole[0], at, first, at, wa)
        copy(whole[1], at, first, at, behind(1))
        copy(whole[2], at, first, at, behind(-1))
        for r in range(2, rounds):
            copy(refs[r - 2], at, first - lo, at, behind(r))
            copy(refs[rounds - 1 + r - 2], at, first - lo, at, behind(-r))
    for at in range(half):
        copy(refs[rounds - 2], at, first - lo, core * half + at, behind(rounds))
        copy(refs[-1], at, first - lo, (1 - core) * half + at, behind(rounds))
    for one in copies:
        one.start()

    def wait():
        for one in copies:
            one.wait()

    return wait


def pack_kernel(conv_ref, up_ref, out_ref):
    for x in range(out_ref.shape[0]):
        lanes = slice(x * LANES, (x + 1) * LANES)
        for a in range(3):
            to = slice(a * LANES, (a + 1) * LANES)
            for b in range(3):
                for k in range(3):
                    out_ref[x, 3 * k + b, :, to] = conv_ref[k, a, b, :, lanes]
                out_ref[x, 9 + b, :, to] = up_ref[a, b, :, lanes]


def slab_kernel(lat_ref, past_ref, cot_ref, left_ref, right_ref, out_ref):
    n_ha, chans = out_ref.shape[0], out_ref.shape[2]
    rows, split = lat_ref.shape[1], lat_ref.shape[0] * lat_ref.shape[1]
    lat = lat_ref[...].astype(F32).reshape(split, lat_ref.shape[2], chans)
    lat = jnp.concatenate(
        [left_ref[:split].astype(F32)[None], jnp.swapaxes(lat, 0, 1), right_ref[:split].astype(F32)[None]], axis=0
    )
    first = jnp.concatenate([lat[:, :rows]] * 2, axis=1)
    past = jnp.where(lax.axis_index("ta") == 0, first, past_ref[...].astype(F32))
    lat = jnp.concatenate([past, lat], axis=1).reshape(-1, chans).astype(BF16)
    for x in range(n_ha):
        out_ref[x, : lat.shape[0]] = lat
    cot = cot_ref[...].astype(F32)
    frames, fine, cols, _ = cot.shape
    points = frames * fine // 2
    cot = cot.reshape(points, 2, cols, chans)
    for odd_row in range(2):
        part = jnp.swapaxes(cot[:, odd_row], 0, 1).astype(BF16)
        edge = slice(split + odd_row * points, split + (odd_row + 1) * points)
        columns = [left_ref[edge], *[part[w] for w in range(cols)], right_ref[edge]]
        for f, column in enumerate(columns):
            rows = pl.ds(lat.shape[0] + f // 2 * points, points)
            to = (f % 2 * 2 + odd_row) * LANES
            for x in range(n_ha):
                out_ref[x, rows, to : to + LANES] = column[:, x * LANES : (x + 1) * LANES]


def up_kernel(slab_ref, *refs):
    *blocks, out_ref, w_ref, rows_ref, sem = refs
    wait = weight_copies(blocks[:3], blocks[3:], 6, 9, 3, 0, w_ref, sem)
    n_ha = slab_ref.shape[0]
    for par in range(2):
        cot = jnp.stack([slab_ref[x, 240:384, :] for x in range(n_ha)], axis=0)
        cot = cot[:, :, 2 * par * LANES : 2 * (par + 1) * LANES].astype(F32)
        cot = jnp.stack([cot[x].reshape(9, 16, 2 * LANES) for x in range(n_ha)], axis=1)
        even, odd = cot[..., :LANES], cot[..., LANES:]
        rows_ref[par, :, :, :, 0:LANES] = odd + from_below(even)
        rows_ref[par, :, :, :, LANES : 2 * LANES] = even + odd
        rows_ref[par, :, :, :, 2 * LANES : 3 * LANES] = even + from_above(odd)
    wait()
    total = None
    for b in range(3):
        box = None
        for e in (1 - b, 2 - b):
            par, off = (e + 1) % 2, (e + 1) // 2
            part = rows_ref[par, off : off + 8]
            box = part if box is None else box + part
        box = box.reshape(-1, 3 * LANES)
        high = box.astype(BF16)
        low = (box - high.astype(F32)).astype(BF16)
        for piece in (high, low):
            term = lax.dot_general(
                piece, w_ref[b], (((1,), (1,)), ((), ())), preferred_element_type=F32
            )
            total = term if total is None else total + term
    for x in range(n_ha):
        out_ref[x] = total[:, x * LANES : (x + 1) * LANES].astype(BF16)


def fwd_kernel(slab_ref, bias_ref, *refs):
    *blocks, out_ref, w_hbm, win_ref, w_ref, sem, out_sem = refs
    whole, early, late = blocks[:3], blocks[3 : 3 + (len(blocks) - 3) // 2], blocks[3 + (len(blocks) - 3) // 2 :]
    early_wait = weight_copies(whole, early, 6, 6, 3, 6, w_ref, sem)
    late_wait = weight_copies(whole, late, 0, 0, 6, 0, w_ref, sem, sem.shape[0] // 2)
    n_ha = slab_ref.shape[0]
    for x in range(n_ha):
        for pair in range(5):
            two = slab_ref[x, pair * 48 : pair * 48 + 48, :].astype(F32)
            for one in range(2):
                for k in range(3):
                    lo = one * 24 + 4 * k
                    win_ref[k, 2 * pair + one, x] = two[lo : lo + 16].astype(BF16)
    early_wait()
    total = None
    for k in (2, 0, 1):
        if k == 0:
            late_wait()
            keep = pltpu.make_async_copy(w_ref, w_hbm, out_sem)
            keep.start()
        for b in range(3):
            window = win_ref[k, b : b + 8].reshape(-1, win_ref.shape[-1])
            term = jnp.dot(window, w_ref[3 * k + b], preferred_element_type=F32)
            total = term if total is None else total + term
    total = total.reshape(8, n_ha, 16, 3 * LANES)
    pre = (
        from_above(total[..., :LANES])
        + total[..., LANES : 2 * LANES]
        + from_below(total[..., 2 * LANES :])
        + bias_ref[...].reshape(1, 1, 1, LANES)
    )
    sig = 1.0 / (1.0 + jnp.exp(-pre))
    out_ref[...] = sig * (1.0 + pre * (1.0 - sig))
    keep.wait()


def gate_kernel(slope_ref, act_ref, out_ref, head_ref, first_ref, last_ref):
    grad = act_ref[0].astype(F32)
    for x in range(1, act_ref.shape[0]):
        grad = grad + act_ref[x].astype(F32)
    grad = (grad.reshape(slope_ref.shape) * slope_ref[...]).astype(BF16)
    out_ref[...] = grad
    first_ref[...] = grad[0]
    last_ref[...] = grad[-1]
    head_ref[...] = grad[:, :, : head_ref.shape[2]]


def bwd_kernel(g_ref, later_ref, left_ref, right_ref, w_hbm, out_ref, win_ref, w_ref, sem):
    fetch = [
        pltpu.make_async_copy(w_hbm.at[pl.ds(3 * k, 3)], w_ref.at[pl.ds(3 * k, 3)], sem.at[k]) for k in range(3)
    ]
    for copy in fetch:
        copy.start()
    n_ha = g_ref.shape[1]
    at_start = (lax.axis_index("ta") == 0).astype(F32)
    grad = jnp.concatenate([g_ref[...].astype(F32), later_ref[...].astype(F32)], axis=2)
    grad = jnp.concatenate(
        [left_ref[...].astype(F32)[None], grad, right_ref[...].astype(F32)[None]], axis=0
    )
    zero, one, two = grad[:, :, 0:4], grad[:, :, 4:8], grad[:, :, 8:12]
    windows = [
        grad[:, :, 0:16],
        jnp.concatenate([one + at_start * zero, grad[:, :, 8:20]], axis=2),
        jnp.concatenate([two + at_start * (zero + one), grad[:, :, 12:24]], axis=2),
    ]
    for shift in range(3):
        x = windows[shift]
        win_ref[shift, :, :, :, 0:LANES] = from_below(x).astype(BF16)
        win_ref[shift, :, :, :, LANES : 2 * LANES] = x.astype(BF16)
        win_ref[shift, :, :, :, 2 * LANES : 3 * LANES] = from_above(x).astype(BF16)
    total = None
    for k in range(3):
        fetch[k].wait()
        for b in range(3):
            window = win_ref[2 - k, 2 - b : 10 - b].reshape(-1, 3 * LANES)
            term = lax.dot_general(
                window, w_ref[3 * k + b], (((1,), (1,)), ((), ())), preferred_element_type=F32
            )
            total = term if total is None else total + term
    total = total.astype(BF16).reshape(8, n_ha, 16, -1)
    for x in range(n_ha):
        out_ref[x] = total[:, x]


def call(kernel, out_shape, specs, scratch, cost=None, outs=None):
    return pl.pallas_call(
        kernel,
        out_shape=out_shape,
        in_specs=specs,
        out_specs=outs or jax.tree.map(lambda _: pl.BlockSpec(memory_space=pltpu.VMEM), out_shape),
        scratch_shapes=scratch,
        cost_estimate=cost,
        compiler_params=pltpu.CompilerParams(vmem_limit_bytes=VMEM_LIMIT),
    )


def in_hbm(x):
    return pltpu.with_memory_space_constraint(x, pltpu.HBM)


def shifted(x, axis, step):
    n = lax.axis_size(axis)
    return lax.ppermute(x, axis, [(i, i + step) for i in range(n) if 0 <= i + step < n])


def on_device(latent, cotangent, conv_bias, conv_weight, up_weight):
    frames, rows, cols, chans = latent.shape
    n_ta, n_ha, n_wa = (lax.axis_size(a) for a in ("ta", "ha", "wa"))
    ta, ha = lax.axis_index("ta"), lax.axis_index("ha")
    shard = conv_weight.shape[3]
    core = lax.rem(ta, 2)

    vmem, anywhere = pl.BlockSpec(memory_space=pltpu.VMEM), pl.BlockSpec(memory_space=pl.ANY)
    groups = call(
        pack_kernel,
        jax.ShapeDtypeStruct((n_ha, 12, shard, 3 * LANES), BF16),
        [vmem, vmem],
        [],
    )(conv_weight, up_weight)
    def edge(col_l, col_c):
        fine = cotangent[:, :, col_c].reshape(frames * rows, 2, chans).transpose(1, 0, 2)
        return jnp.concatenate([latent[:, :, col_l].reshape(-1, chans), fine.reshape(-1, chans)], axis=0)

    left = shifted(edge(cols - 1, 2 * cols - 1), "wa", 1)
    right = shifted(edge(0, 0), "wa", -1)
    tail = slice((frames - 2) * rows, frames * rows)
    middle = latent[frames - 2 :].transpose(2, 0, 1, 3).reshape(cols, 2 * rows, chans)
    past = shifted(jnp.concatenate([left[None, tail], middle, right[None, tail]], axis=0), "ta", 1)
    groups, past = lax.optimization_barrier((lax.all_to_all(groups, "ha", 0, 0), past))
    length = (cols + 2) * (frames + 2) * rows + (cols + 1) * frames * rows
    slab = call(
        slab_kernel, jax.ShapeDtypeStruct((n_ha, length, chans), BF16), [vmem] * 5, []
    )(latent, past, cotangent, left, right)

    swap = [(i, i ^ 1) for i in range(n_ta)]
    around = [
        (t * n_wa + (w + 1 - 2 * (t % 2)) % n_wa, t * n_wa + w) for t in range(n_ta) for w in range(n_wa)
    ]
    spans = [(6, 12), (0, 6)]
    block, slab = lax.optimization_barrier((lax.ppermute(groups, ("ta", "wa"), around), slab))
    swapped = lax.ppermute(block, "ta", swap)
    mine, others = [], []
    for lo, hi in spans:
        mine.append([block[:, lo:hi]])
        others.append([])
    for r in range(2, n_wa // 2 + 1):
        for q in range(2):
            part = mine[q][-1]
            if r == n_wa // 2:
                part = lax.dynamic_slice_in_dim(part, core * (n_ha // 2), n_ha // 2, axis=0)
            mine[q].append(lax.ppermute(part, ("ta", "wa"), around))
            others[q].append(lax.ppermute(mine[q][-1], "ta", swap))
    whole = [groups, block, swapped]
    slab = lax.all_to_all(slab, "ha", 0, 0)
    early, late = mine[0][1:] + others[0], mine[1][1:] + others[1]

    points = cols * n_ha * frames * rows
    copies = (n_wa - 1) * n_ha + n_ha
    dma = pltpu.SemaphoreType.DMA
    act = call(
        up_kernel,
        jax.ShapeDtypeStruct((n_ha, points, LANES), BF16),
        [vmem] + [anywhere] * len(whole + early),
        [
            pltpu.VMEM((3, chans, 3 * LANES), BF16),
            pltpu.VMEM((2, cols + 1, n_ha, frames * rows, 3 * LANES), F32),
            dma((copies,)),
        ],
    )(slab, *[in_hbm(x) for x in whole + early])
    act = lax.all_to_all(act, "ha", 0, 0)

    bias = lax.dynamic_slice_in_dim(conv_bias, ha * LANES, LANES).reshape(1, LANES)
    hbm = pl.BlockSpec(memory_space=pltpu.HBM)
    w_conv = (9, chans, 3 * LANES)
    slope, w_conv = call(
        fwd_kernel,
        (jax.ShapeDtypeStruct((cols, n_ha, frames * rows, LANES), F32), pltpu.HBM(w_conv, BF16)),
        [vmem, vmem] + [anywhere] * len(whole + early + late),
        [
            pltpu.VMEM((3, cols + 2, n_ha, frames * rows, chans), BF16),
            pltpu.VMEM(w_conv, BF16),
            dma((2 * copies,)),
            dma,
        ],
        pl.CostEstimate(flops=3 * 9 * 2 * points * LANES * chans, bytes_accessed=5 << 20, transcendentals=0),
        (vmem, hbm),
    )(slab, bias, *[in_hbm(x) for x in whole + early + late])
    w_conv = in_hbm(w_conv)
    deep, high = frames * rows, 2 * rows
    shapes = [(cols, n_ha, deep), (cols, n_ha, high), (n_ha, deep), (n_ha, deep)]
    grad, head, first, last = call(
        gate_kernel, [jax.ShapeDtypeStruct((*sh, LANES), BF16) for sh in shapes], [vmem, vmem], []
    )(slope, act)

    later = shifted(head, "ta", -1)
    g_left = shifted(jnp.concatenate([last, later[cols - 1]], axis=1), "wa", 1)
    g_right = shifted(jnp.concatenate([first, later[0]], axis=1), "wa", -1)

    out = call(
        bwd_kernel,
        jax.ShapeDtypeStruct((n_ha, cols, frames * rows, chans), BF16),
        [vmem, vmem, vmem, vmem, hbm],
        [pltpu.VMEM((3, cols + 2, n_ha, frames * rows, 3 * LANES), BF16), pltpu.VMEM(w_conv.shape, BF16), dma((3,))],
    )(grad, later, g_left, g_right, w_conv)
    out = lax.all_to_all(out, "ha", 0, 0)
    out = out.astype(F32).sum(axis=0).reshape(cols, frames, rows, chans)
    return out.transpose(1, 2, 0, 3).astype(BF16)


def solution(mesh):
    in_specs = (
        P("ta", "ha", "wa", None),
        P("ta", "ha", "wa", None),
        P(),
        P(None, None, None, ("ha", "wa"), None),
        P(None, None, ("ha", "wa"), None),
    )
    return jax.shard_map(
        on_device, mesh=mesh, in_specs=in_specs, out_specs=P("ta", "ha", "wa", None), check_vma=False
    )
```

```python
import functools

import jax
import jax.numpy as jnp
from jax import lax
from jax.experimental import pallas as pl
from jax.experimental.pallas import tpu as pltpu
from jax.sharding import PartitionSpec as P

F32, BF16 = jnp.float32, jnp.bfloat16
LANES = 128
VMEM_LIMIT = 24 * 1024 * 1024


def roll_rows(x, shift):
    return pltpu.roll(x, shift, x.ndim - 2)


def row_in_block(shape):
    return lax.broadcasted_iota(jnp.int32, shape, len(shape) - 2) % 4


def from_above(x):
    prev = jnp.concatenate([jnp.zeros_like(x[:, :1]), x[:, :-1]], axis=1)
    n = x.shape[2]
    return jnp.where(row_in_block(x.shape) == 0, roll_rows(prev, n - 3), roll_rows(x, 1))


def from_below(x):
    later = jnp.concatenate([x[:, 1:], jnp.zeros_like(x[:, :1])], axis=1)
    n = x.shape[2]
    return jnp.where(row_in_block(x.shape) == 3, roll_rows(later, 3), roll_rows(x, n - 1))


def weight_copies(whole, refs, lo, first, groups, to, w_ref, sem, base=0):
    core = lax.rem(lax.axis_index("ta"), 2)
    wa = lax.axis_index("wa")
    way = 1 - 2 * core
    rounds = len(refs) // 2 + 1
    n_wa, (n_ha, _, shard, _) = 2 * rounds, whole[0].shape
    half = n_ha // 2
    copies = []

    def copy(ref, at, begin, ha, place):
        row = pl.multiple_of((ha * n_wa + place) * shard, shard)
        copies.append(
            pltpu.make_async_copy(
                ref.at[at, pl.ds(begin, groups)],
                w_ref.at[pl.ds(to, groups), pl.ds(row, shard)],
                sem.at[base + len(copies)],
            )
        )

    def behind(r):
        return lax.rem(wa + n_wa + way * r, n_wa)

    for at in range(n_ha):
        copy(whole[0], at, first, at, wa)
        copy(whole[1], at, first, at, behind(1))
        copy(whole[2], at, first, at, behind(-1))
        for r in range(2, rounds):
            copy(refs[r - 2], at, first - lo, at, behind(r))
            copy(refs[rounds - 1 + r - 2], at, first - lo, at, behind(-r))
    for at in range(half):
        copy(refs[rounds - 2], at, first - lo, core * half + at, behind(rounds))
        copy(refs[-1], at, first - lo, (1 - core) * half + at, behind(rounds))
    for one in copies:
        one.start()

    def wait():
        for one in copies:
            one.wait()

    return wait


def pack_kernel(conv_ref, up_ref, out_ref):
    for x in range(out_ref.shape[0]):
        lanes = slice(x * LANES, (x + 1) * LANES)
        for a in range(3):
            to = slice(a * LANES, (a + 1) * LANES)
            for b in range(3):
                for k in range(3):
                    out_ref[x, 3 * k + b, :, to] = conv_ref[k, a, b, :, lanes]
                out_ref[x, 9 + b, :, to] = up_ref[a, b, :, lanes]


def slab_kernel(lat_ref, past_ref, cot_ref, left_ref, right_ref, out_ref):
    n_ha, chans = out_ref.shape[0], out_ref.shape[2]
    rows, split = lat_ref.shape[1], lat_ref.shape[0] * lat_ref.shape[1]
    lat = lat_ref[...].astype(F32).reshape(split, lat_ref.shape[2], chans)
    lat = jnp.concatenate(
        [left_ref[:split].astype(F32)[None], jnp.swapaxes(lat, 0, 1), right_ref[:split].astype(F32)[None]], axis=0
    )
    first = jnp.concatenate([lat[:, :rows]] * 2, axis=1)
    past = jnp.where(lax.axis_index("ta") == 0, first, past_ref[...].astype(F32))
    lat = jnp.concatenate([past, lat], axis=1).reshape(-1, chans).astype(BF16)
    for x in range(n_ha):
        out_ref[x, : lat.shape[0]] = lat
    cot = cot_ref[...].astype(F32)
    frames, fine, cols, _ = cot.shape
    points = frames * fine // 2
    cot = cot.reshape(points, 2, cols, chans)
    for odd_row in range(2):
        part = jnp.swapaxes(cot[:, odd_row], 0, 1).astype(BF16)
        edge = slice(split + odd_row * points, split + (odd_row + 1) * points)
        columns = [left_ref[edge], *[part[w] for w in range(cols)], right_ref[edge]]
        for f, column in enumerate(columns):
            rows = pl.ds(lat.shape[0] + f // 2 * points, points)
            to = (f % 2 * 2 + odd_row) * LANES
            for x in range(n_ha):
                out_ref[x, rows, to : to + LANES] = column[:, x * LANES : (x + 1) * LANES]


def up_kernel(slab_ref, *refs):
    *blocks, out_ref, w_ref, rows_ref, sem = refs
    wait = weight_copies(blocks[:3], blocks[3:], 6, 9, 3, 0, w_ref, sem)
    n_ha = slab_ref.shape[0]
    for par in range(2):
        cot = jnp.stack([slab_ref[x, 240:384, :] for x in range(n_ha)], axis=0)
        cot = cot[:, :, 2 * par * LANES : 2 * (par + 1) * LANES].astype(F32)
        cot = jnp.stack([cot[x].reshape(9, 16, 2 * LANES) for x in range(n_ha)], axis=1)
        even, odd = cot[..., :LANES], cot[..., LANES:]
        rows_ref[par, :, :, :, 0:LANES] = odd + from_below(even)
        rows_ref[par, :, :, :, LANES : 2 * LANES] = even + odd
        rows_ref[par, :, :, :, 2 * LANES : 3 * LANES] = even + from_above(odd)
    wait()
    total = None
    for b in range(3):
        box = None
        for e in (1 - b, 2 - b):
            par, off = (e + 1) % 2, (e + 1) // 2
            part = rows_ref[par, off : off + 8]
            box = part if box is None else box + part
        box = box.reshape(-1, 3 * LANES)
        high = box.astype(BF16)
        low = (box - high.astype(F32)).astype(BF16)
        term = lax.dot_general(
            jnp.concatenate([high, low], axis=1),
            jnp.concatenate([w_ref[b], w_ref[b]], axis=1),
            (((1,), (1,)), ((), ())),
            preferred_element_type=F32,
        )
        total = term if total is None else total + term
    for x in range(n_ha):
        out_ref[x] = total[:, x * LANES : (x + 1) * LANES].astype(BF16)


def fwd_kernel(slab_ref, bias_ref, *refs):
    *blocks, out_ref, w_hbm, win_ref, w_ref, sem, out_sem = refs
    whole, early, late = blocks[:3], blocks[3 : 3 + (len(blocks) - 3) // 2], blocks[3 + (len(blocks) - 3) // 2 :]
    early_wait = weight_copies(whole, early, 6, 6, 3, 6, w_ref, sem)
    late_wait = weight_copies(whole, late, 0, 0, 6, 0, w_ref, sem, sem.shape[0] // 2)
    n_ha = slab_ref.shape[0]
    for x in range(n_ha):
        for pair in range(5):
            two = slab_ref[x, pair * 48 : pair * 48 + 48, :].astype(F32)
            for one in range(2):
                for k in range(3):
                    lo = one * 24 + 4 * k
                    win_ref[k, 2 * pair + one, x] = two[lo : lo + 16].astype(BF16)
    early_wait()
    total = None
    for k in (2, 0, 1):
        if k == 0:
            late_wait()
            keep = pltpu.make_async_copy(w_ref, w_hbm, out_sem)
            keep.start()
        for b in range(3):
            window = win_ref[k, b : b + 8].reshape(-1, win_ref.shape[-1])
            term = jnp.dot(window, w_ref[3 * k + b], preferred_element_type=F32)
            total = term if total is None else total + term
    total = total.reshape(8, n_ha, 16, 3 * LANES)
    pre = (
        from_above(total[..., :LANES])
        + total[..., LANES : 2 * LANES]
        + from_below(total[..., 2 * LANES :])
        + bias_ref[...].reshape(1, 1, 1, LANES)
    )
    sig = 1.0 / (1.0 + jnp.exp(-pre))
    out_ref[...] = sig * (1.0 + pre * (1.0 - sig))
    keep.wait()


def gate_kernel(slope_ref, act_ref, out_ref, head_ref, first_ref, last_ref):
    grad = act_ref[0].astype(F32)
    for x in range(1, act_ref.shape[0]):
        grad = grad + act_ref[x].astype(F32)
    grad = (grad.reshape(slope_ref.shape) * slope_ref[...]).astype(BF16)
    out_ref[...] = grad
    first_ref[...] = grad[0]
    last_ref[...] = grad[-1]
    head_ref[...] = grad[:, :, : head_ref.shape[2]]


def bwd_kernel(g_ref, later_ref, left_ref, right_ref, w_hbm, out_ref, win_ref, w_ref, sem):
    fetch = [
        pltpu.make_async_copy(w_hbm.at[pl.ds(3 * k, 3)], w_ref.at[pl.ds(3 * k, 3)], sem.at[k]) for k in range(3)
    ]
    for copy in fetch:
        copy.start()
    n_ha = g_ref.shape[1]
    at_start = (lax.axis_index("ta") == 0).astype(F32)
    grad = jnp.concatenate([g_ref[...].astype(F32), later_ref[...].astype(F32)], axis=2)
    grad = jnp.concatenate(
        [left_ref[...].astype(F32)[None], grad, right_ref[...].astype(F32)[None]], axis=0
    )
    zero, one, two = grad[:, :, 0:4], grad[:, :, 4:8], grad[:, :, 8:12]
    windows = [
        grad[:, :, 0:16],
        jnp.concatenate([one + at_start * zero, grad[:, :, 8:20]], axis=2),
        jnp.concatenate([two + at_start * (zero + one), grad[:, :, 12:24]], axis=2),
    ]
    for shift in range(3):
        x = windows[shift]
        win_ref[shift, :, :, :, 0:LANES] = from_below(x).astype(BF16)
        win_ref[shift, :, :, :, LANES : 2 * LANES] = x.astype(BF16)
        win_ref[shift, :, :, :, 2 * LANES : 3 * LANES] = from_above(x).astype(BF16)
    total = None
    taps = [(k, b) for k in range(3) for b in range(3)]
    for few in (taps[0:2], taps[2:4], taps[4:6], taps[6:8], taps[8:9]):
        for k, b in few:
            if b == 0:
                fetch[k].wait()
        term = lax.dot_general(
            jnp.concatenate([win_ref[2 - k, 2 - b : 10 - b].reshape(-1, 3 * LANES) for k, b in few], axis=1),
            jnp.concatenate([w_ref[3 * k + b] for k, b in few], axis=1),
            (((1,), (1,)), ((), ())),
            preferred_element_type=F32,
        )
        total = term if total is None else total + term
    total = total.astype(BF16).reshape(8, n_ha, 16, -1)
    for x in range(n_ha):
        out_ref[x] = total[:, x]


def call(kernel, out_shape, specs, scratch, cost=None, outs=None):
    return pl.pallas_call(
        kernel,
        out_shape=out_shape,
        in_specs=specs,
        out_specs=outs or jax.tree.map(lambda _: pl.BlockSpec(memory_space=pltpu.VMEM), out_shape),
        scratch_shapes=scratch,
        cost_estimate=cost,
        compiler_params=pltpu.CompilerParams(vmem_limit_bytes=VMEM_LIMIT),
    )


def in_hbm(x):
    return pltpu.with_memory_space_constraint(x, pltpu.HBM)


def shifted(x, axis, step):
    n = lax.axis_size(axis)
    return lax.ppermute(x, axis, [(i, i + step) for i in range(n) if 0 <= i + step < n])


def on_device(latent, cotangent, conv_bias, conv_weight, up_weight):
    frames, rows, cols, chans = latent.shape
    n_ta, n_ha, n_wa = (lax.axis_size(a) for a in ("ta", "ha", "wa"))
    ta, ha = lax.axis_index("ta"), lax.axis_index("ha")
    shard = conv_weight.shape[3]
    core = lax.rem(ta, 2)

    vmem, anywhere = pl.BlockSpec(memory_space=pltpu.VMEM), pl.BlockSpec(memory_space=pl.ANY)
    groups = call(
        pack_kernel,
        jax.ShapeDtypeStruct((n_ha, 12, shard, 3 * LANES), BF16),
        [vmem, vmem],
        [],
    )(conv_weight, up_weight)
    def edge(col_l, col_c):
        fine = cotangent[:, :, col_c].reshape(frames * rows, 2, chans).transpose(1, 0, 2)
        return jnp.concatenate([latent[:, :, col_l].reshape(-1, chans), fine.reshape(-1, chans)], axis=0)

    left = shifted(edge(cols - 1, 2 * cols - 1), "wa", 1)
    right = shifted(edge(0, 0), "wa", -1)
    tail = slice((frames - 2) * rows, frames * rows)
    middle = latent[frames - 2 :].transpose(2, 0, 1, 3).reshape(cols, 2 * rows, chans)
    past = shifted(jnp.concatenate([left[None, tail], middle, right[None, tail]], axis=0), "ta", 1)
    groups = lax.all_to_all(groups, "ha", 0, 0)
    length = (cols + 2) * (frames + 2) * rows + (cols + 1) * frames * rows
    slab = call(
        slab_kernel, jax.ShapeDtypeStruct((n_ha, length, chans), BF16), [vmem] * 5, []
    )(latent, past, cotangent, left, right)

    swap = [(i, i ^ 1) for i in range(n_ta)]
    around = [
        (t * n_wa + (w + 1 - 2 * (t % 2)) % n_wa, t * n_wa + w) for t in range(n_ta) for w in range(n_wa)
    ]
    spans = [(6, 12), (0, 6)]
    block = lax.ppermute(groups, ("ta", "wa"), around)
    swapped = lax.ppermute(block, "ta", swap)
    mine, others = [], []
    for lo, hi in spans:
        mine.append([block[:, lo:hi]])
        others.append([])
    for r in range(2, n_wa // 2 + 1):
        for q in range(2):
            part = mine[q][-1]
            if r == n_wa // 2:
                part = lax.dynamic_slice_in_dim(part, core * (n_ha // 2), n_ha // 2, axis=0)
            mine[q].append(lax.ppermute(part, ("ta", "wa"), around))
            others[q].append(lax.ppermute(mine[q][-1], "ta", swap))
    whole = [groups, block, swapped]
    slab = lax.all_to_all(slab, "ha", 0, 0)
    early, late = mine[0][1:] + others[0], mine[1][1:] + others[1]

    points = cols * n_ha * frames * rows
    copies = (n_wa - 1) * n_ha + n_ha
    dma = pltpu.SemaphoreType.DMA
    act = call(
        up_kernel,
        jax.ShapeDtypeStruct((n_ha, points, LANES), BF16),
        [vmem] + [anywhere] * len(whole + early),
        [
            pltpu.VMEM((3, chans, 3 * LANES), BF16),
            pltpu.VMEM((2, cols + 1, n_ha, frames * rows, 3 * LANES), F32),
            dma((copies,)),
        ],
    )(slab, *[in_hbm(x) for x in whole + early])
    act = lax.all_to_all(act, "ha", 0, 0)

    bias = lax.dynamic_slice_in_dim(conv_bias, ha * LANES, LANES).reshape(1, LANES)
    hbm = pl.BlockSpec(memory_space=pltpu.HBM)
    w_conv = (9, chans, 3 * LANES)
    slope, w_conv = call(
        fwd_kernel,
        (jax.ShapeDtypeStruct((cols, n_ha, frames * rows, LANES), F32), pltpu.HBM(w_conv, BF16)),
        [vmem, vmem] + [anywhere] * len(whole + early + late),
        [
            pltpu.VMEM((3, cols + 2, n_ha, frames * rows, chans), BF16),
            pltpu.VMEM(w_conv, BF16),
            dma((2 * copies,)),
            dma,
        ],
        pl.CostEstimate(flops=3 * 9 * 2 * points * LANES * chans, bytes_accessed=5 << 20, transcendentals=0),
        (vmem, hbm),
    )(slab, bias, *[in_hbm(x) for x in whole + early + late])
    w_conv = in_hbm(w_conv)
    deep, high = frames * rows, 2 * rows
    shapes = [(cols, n_ha, deep), (cols, n_ha, high), (n_ha, deep), (n_ha, deep)]
    grad, head, first, last = call(
        gate_kernel, [jax.ShapeDtypeStruct((*sh, LANES), BF16) for sh in shapes], [vmem, vmem], []
    )(slope, act)

    later = shifted(head, "ta", -1)
    g_left = shifted(jnp.concatenate([last, later[cols - 1]], axis=1), "wa", 1)
    g_right = shifted(jnp.concatenate([first, later[0]], axis=1), "wa", -1)

    out = call(
        bwd_kernel,
        jax.ShapeDtypeStruct((n_ha, cols, frames * rows, chans), BF16),
        [vmem, vmem, vmem, vmem, hbm],
        [pltpu.VMEM((3, cols + 2, n_ha, frames * rows, 3 * LANES), BF16), pltpu.VMEM(w_conv.shape, BF16), dma((3,))],
    )(grad, later, g_left, g_right, w_conv)
    out = lax.all_to_all(out, "ha", 0, 0)
    out = out.astype(F32).sum(axis=0).reshape(cols, frames, rows, chans)
    return out.transpose(1, 2, 0, 3).astype(BF16)


def solution(mesh):
    in_specs = (
        P("ta", "ha", "wa", None),
        P("ta", "ha", "wa", None),
        P(),
        P(None, None, None, ("ha", "wa"), None),
        P(None, None, ("ha", "wa"), None),
    )
    return jax.shard_map(
        on_device, mesh=mesh, in_specs=in_specs, out_specs=P("ta", "ha", "wa", None), check_vma=False
    )
```

```python
import functools

import jax
import jax.numpy as jnp
from jax import lax
from jax.experimental import pallas as pl
from jax.experimental.pallas import tpu as pltpu
from jax.sharding import PartitionSpec as P

F32, BF16 = jnp.float32, jnp.bfloat16
LANES = 128
VMEM_LIMIT = 24 * 1024 * 1024


def roll_rows(x, shift):
    return pltpu.roll(x, shift, x.ndim - 2)


def row_in_block(shape):
    return lax.broadcasted_iota(jnp.int32, shape, len(shape) - 2) % 4


def from_above(x):
    prev = jnp.concatenate([jnp.zeros_like(x[:, :1]), x[:, :-1]], axis=1)
    n = x.shape[2]
    return jnp.where(row_in_block(x.shape) == 0, roll_rows(prev, n - 3), roll_rows(x, 1))


def from_below(x):
    later = jnp.concatenate([x[:, 1:], jnp.zeros_like(x[:, :1])], axis=1)
    n = x.shape[2]
    return jnp.where(row_in_block(x.shape) == 3, roll_rows(later, 3), roll_rows(x, n - 1))


def weight_copies(whole, refs, lo, first, groups, to, w_ref, sem, base=0):
    core = lax.rem(lax.axis_index("ta"), 2)
    wa = lax.axis_index("wa")
    way = 1 - 2 * core
    rounds = len(refs) // 2 + 1
    n_wa, (n_ha, _, shard, _) = 2 * rounds, whole[0].shape
    half = n_ha // 2
    copies = []

    def copy(ref, at, begin, ha, place):
        row = pl.multiple_of((ha * n_wa + place) * shard, shard)
        copies.append(
            pltpu.make_async_copy(
                ref.at[at, pl.ds(begin, groups)],
                w_ref.at[pl.ds(to, groups), pl.ds(row, shard)],
                sem.at[base + len(copies)],
            )
        )

    def behind(r):
        return lax.rem(wa + n_wa + way * r, n_wa)

    for at in range(n_ha):
        copy(whole[0], at, first, at, wa)
        copy(whole[1], at, first, at, behind(1))
        copy(whole[2], at, first, at, behind(-1))
        for r in range(2, rounds):
            copy(refs[r - 2], at, first - lo, at, behind(r))
            copy(refs[rounds - 1 + r - 2], at, first - lo, at, behind(-r))
    for at in range(half):
        copy(refs[rounds - 2], at, first - lo, core * half + at, behind(rounds))
        copy(refs[-1], at, first - lo, (1 - core) * half + at, behind(rounds))
    for one in copies:
        one.start()

    def wait():
        for one in copies:
            one.wait()

    return wait


def pack_kernel(conv_ref, up_ref, out_ref):
    for x in range(out_ref.shape[0]):
        lanes = slice(x * LANES, (x + 1) * LANES)
        for a in range(3):
            to = slice(a * LANES, (a + 1) * LANES)
            for b in range(3):
                for k in range(3):
                    out_ref[x, 3 * k + b, :, to] = conv_ref[k, a, b, :, lanes]
                out_ref[x, 9 + b, :, to] = up_ref[a, b, :, lanes]


def slab_kernel(lat_ref, past_ref, cot_ref, left_ref, right_ref, out_ref):
    n_ha, chans = out_ref.shape[0], out_ref.shape[2]
    rows, split = lat_ref.shape[1], lat_ref.shape[0] * lat_ref.shape[1]
    lat = lat_ref[...].astype(F32).reshape(split, lat_ref.shape[2], chans)
    lat = jnp.concatenate(
        [left_ref[:split].astype(F32)[None], jnp.swapaxes(lat, 0, 1), right_ref[:split].astype(F32)[None]], axis=0
    )
    first = jnp.concatenate([lat[:, :rows]] * 2, axis=1)
    past = jnp.where(lax.axis_index("ta") == 0, first, past_ref[...].astype(F32))
    lat = jnp.concatenate([past, lat], axis=1).reshape(-1, chans).astype(BF16)
    for x in range(n_ha):
        out_ref[x, : lat.shape[0]] = lat
    cot = cot_ref[...].astype(F32)
    frames, fine, cols, _ = cot.shape
    points = frames * fine // 2
    cot = cot.reshape(points, 2, cols, chans)
    for odd_row in range(2):
        part = jnp.swapaxes(cot[:, odd_row], 0, 1).astype(BF16)
        edge = slice(split + odd_row * points, split + (odd_row + 1) * points)
        columns = [left_ref[edge], *[part[w] for w in range(cols)], right_ref[edge]]
        for f, column in enumerate(columns):
            rows = pl.ds(lat.shape[0] + f // 2 * points, points)
            to = (f % 2 * 2 + odd_row) * LANES
            for x in range(n_ha):
                out_ref[x, rows, to : to + LANES] = column[:, x * LANES : (x + 1) * LANES]


def up_kernel(slab_ref, *refs):
    *blocks, out_ref, w_ref, rows_ref, sem = refs
    wait = weight_copies(blocks[:3], blocks[3:], 6, 9, 3, 0, w_ref, sem)
    n_ha = slab_ref.shape[0]
    for par in range(2):
        cot = jnp.stack([slab_ref[x, 240:384, :] for x in range(n_ha)], axis=0)
        cot = cot[:, :, 2 * par * LANES : 2 * (par + 1) * LANES].astype(F32)
        cot = jnp.stack([cot[x].reshape(9, 16, 2 * LANES) for x in range(n_ha)], axis=1)
        even, odd = cot[..., :LANES], cot[..., LANES:]
        rows_ref[par, :, :, :, 0:LANES] = odd + from_below(even)
        rows_ref[par, :, :, :, LANES : 2 * LANES] = even + odd
        rows_ref[par, :, :, :, 2 * LANES : 3 * LANES] = even + from_above(odd)
    wait()
    total = None
    for b in range(3):
        box = None
        for e in (1 - b, 2 - b):
            par, off = (e + 1) % 2, (e + 1) // 2
            part = rows_ref[par, off : off + 8]
            box = part if box is None else box + part
        box = box.reshape(-1, 3 * LANES)
        high = box.astype(BF16)
        low = (box - high.astype(F32)).astype(BF16)
        term = lax.dot_general(
            jnp.concatenate([high, low], axis=1),
            jnp.concatenate([w_ref[b], w_ref[b]], axis=1),
            (((1,), (1,)), ((), ())),
            preferred_element_type=F32,
        )
        total = term if total is None else total + term
    for x in range(n_ha):
        out_ref[x] = total[:, x * LANES : (x + 1) * LANES].astype(BF16)


def fwd_kernel(slab_ref, bias_ref, *refs):
    *blocks, out_ref, w_hbm, win_ref, w_ref, sem, out_sem = refs
    whole, early, late = blocks[:3], blocks[3 : 3 + (len(blocks) - 3) // 2], blocks[3 + (len(blocks) - 3) // 2 :]
    early_wait = weight_copies(whole, early, 6, 6, 3, 6, w_ref, sem)
    late_wait = weight_copies(whole, late, 0, 0, 6, 0, w_ref, sem, sem.shape[0] // 2)
    n_ha = slab_ref.shape[0]
    for x in range(n_ha):
        for pair in range(5):
            two = slab_ref[x, pair * 48 : pair * 48 + 48, :].astype(F32)
            for one in range(2):
                for k in range(3):
                    lo = one * 24 + 4 * k
                    win_ref[k, 2 * pair + one, x] = two[lo : lo + 16].astype(BF16)
    early_wait()
    total = None
    for k in (2, 0, 1):
        if k == 0:
            late_wait()
            keep = pltpu.make_async_copy(w_ref, w_hbm, out_sem)
            keep.start()
        for b in range(3):
            window = win_ref[k, b : b + 8].reshape(-1, win_ref.shape[-1])
            term = jnp.dot(window, w_ref[3 * k + b], preferred_element_type=F32)
            total = term if total is None else total + term
    total = total.reshape(8, n_ha, 16, 3 * LANES)
    pre = (
        from_above(total[..., :LANES])
        + total[..., LANES : 2 * LANES]
        + from_below(total[..., 2 * LANES :])
        + bias_ref[...].reshape(1, 1, 1, LANES)
    )
    sig = 1.0 / (1.0 + jnp.exp(-pre))
    out_ref[...] = sig * (1.0 + pre * (1.0 - sig))
    keep.wait()


def gate_kernel(slope_ref, act_ref, out_ref, head_ref, first_ref, last_ref):
    grad = act_ref[0].astype(F32)
    for x in range(1, act_ref.shape[0]):
        grad = grad + act_ref[x].astype(F32)
    grad = (grad.reshape(slope_ref.shape) * slope_ref[...]).astype(BF16)
    out_ref[...] = grad
    first_ref[...] = grad[0]
    last_ref[...] = grad[-1]
    head_ref[...] = grad[:, :, : head_ref.shape[2]]


def bwd_kernel(g_ref, later_ref, left_ref, right_ref, w_hbm, out_ref, win_ref, w_ref, sem):
    fetch = [
        pltpu.make_async_copy(w_hbm.at[pl.ds(3 * k, 3)], w_ref.at[pl.ds(3 * k, 3)], sem.at[k]) for k in range(3)
    ]
    for copy in fetch:
        copy.start()
    n_ha = g_ref.shape[1]
    at_start = (lax.axis_index("ta") == 0).astype(F32)
    grad = jnp.concatenate([g_ref[...].astype(F32), later_ref[...].astype(F32)], axis=2)
    grad = jnp.concatenate(
        [left_ref[...].astype(F32)[None], grad, right_ref[...].astype(F32)[None]], axis=0
    )
    zero, one, two = grad[:, :, 0:4], grad[:, :, 4:8], grad[:, :, 8:12]
    windows = [
        grad[:, :, 0:16],
        jnp.concatenate([one + at_start * zero, grad[:, :, 8:20]], axis=2),
        jnp.concatenate([two + at_start * (zero + one), grad[:, :, 12:24]], axis=2),
    ]
    for shift in range(3):
        x = windows[shift]
        win_ref[shift, :, :, :, 0:LANES] = from_below(x).astype(BF16)
        win_ref[shift, :, :, :, LANES : 2 * LANES] = x.astype(BF16)
        win_ref[shift, :, :, :, 2 * LANES : 3 * LANES] = from_above(x).astype(BF16)
    total = None
    taps = [(k, b) for k in range(3) for b in range(3)]
    for few in (taps[0:2], taps[2:4], taps[4:6], taps[6:8], taps[8:9]):
        for k, b in few:
            if b == 0:
                fetch[k].wait()
        term = lax.dot_general(
            jnp.concatenate([win_ref[2 - k, 2 - b : 10 - b].reshape(-1, 3 * LANES) for k, b in few], axis=1),
            jnp.concatenate([w_ref[3 * k + b] for k, b in few], axis=1),
            (((1,), (1,)), ((), ())),
            preferred_element_type=F32,
        )
        total = term if total is None else total + term
    total = total.astype(BF16).reshape(8, n_ha, 16, -1)
    for x in range(n_ha):
        out_ref[x] = total[:, x]


def call(kernel, out_shape, specs, scratch, cost=None, outs=None):
    return pl.pallas_call(
        kernel,
        out_shape=out_shape,
        in_specs=specs,
        out_specs=outs or jax.tree.map(lambda _: pl.BlockSpec(memory_space=pltpu.VMEM), out_shape),
        scratch_shapes=scratch,
        cost_estimate=cost,
        compiler_params=pltpu.CompilerParams(vmem_limit_bytes=VMEM_LIMIT),
    )


def in_hbm(x):
    return pltpu.with_memory_space_constraint(x, pltpu.HBM)


def settled(blocks):
    return [x if x.shape[0] == 2 else in_hbm(x) for x in blocks]


def shifted(x, axis, step):
    n = lax.axis_size(axis)
    return lax.ppermute(x, axis, [(i, i + step) for i in range(n) if 0 <= i + step < n])


def on_device(latent, cotangent, conv_bias, conv_weight, up_weight):
    frames, rows, cols, chans = latent.shape
    n_ta, n_ha, n_wa = (lax.axis_size(a) for a in ("ta", "ha", "wa"))
    ta, ha = lax.axis_index("ta"), lax.axis_index("ha")
    shard = conv_weight.shape[3]
    core = lax.rem(ta, 2)

    vmem, anywhere = pl.BlockSpec(memory_space=pltpu.VMEM), pl.BlockSpec(memory_space=pl.ANY)
    groups = call(
        pack_kernel,
        jax.ShapeDtypeStruct((n_ha, 12, shard, 3 * LANES), BF16),
        [vmem, vmem],
        [],
    )(in_hbm(conv_weight), in_hbm(up_weight))
    def edge(col_l, col_c):
        fine = cotangent[:, :, col_c].reshape(frames * rows, 2, chans).transpose(1, 0, 2)
        return jnp.concatenate([latent[:, :, col_l].reshape(-1, chans), fine.reshape(-1, chans)], axis=0)

    left = shifted(edge(cols - 1, 2 * cols - 1), "wa", 1)
    right = shifted(edge(0, 0), "wa", -1)
    tail = slice((frames - 2) * rows, frames * rows)
    middle = latent[frames - 2 :].transpose(2, 0, 1, 3).reshape(cols, 2 * rows, chans)
    past = shifted(jnp.concatenate([left[None, tail], middle, right[None, tail]], axis=0), "ta", 1)
    groups = lax.all_to_all(groups, "ha", 0, 0)
    length = (cols + 2) * (frames + 2) * rows + (cols + 1) * frames * rows
    slab = call(
        slab_kernel, jax.ShapeDtypeStruct((n_ha, length, chans), BF16), [vmem] * 5, []
    )(latent, past, cotangent, left, right)

    swap = [(i, i ^ 1) for i in range(n_ta)]
    around = [
        (t * n_wa + (w + 1 - 2 * (t % 2)) % n_wa, t * n_wa + w) for t in range(n_ta) for w in range(n_wa)
    ]
    spans = [(6, 12), (0, 6)]
    block = lax.ppermute(groups, ("ta", "wa"), around)
    swapped = lax.ppermute(block, "ta", swap)
    mine, others = [], []
    for lo, hi in spans:
        mine.append([block[:, lo:hi]])
        others.append([])
    for r in range(2, n_wa // 2 + 1):
        for q in range(2):
            part = mine[q][-1]
            if r == n_wa // 2:
                part = lax.dynamic_slice_in_dim(part, core * (n_ha // 2), n_ha // 2, axis=0)
            mine[q].append(lax.ppermute(part, ("ta", "wa"), around))
            others[q].append(lax.ppermute(mine[q][-1], "ta", swap))
    whole = [groups, block, swapped]
    slab = lax.all_to_all(slab, "ha", 0, 0)
    early, late = mine[0][1:] + others[0], mine[1][1:] + others[1]

    points = cols * n_ha * frames * rows
    copies = (n_wa - 1) * n_ha + n_ha
    dma = pltpu.SemaphoreType.DMA
    act = call(
        up_kernel,
        jax.ShapeDtypeStruct((n_ha, points, LANES), BF16),
        [vmem] + [anywhere] * len(whole + early),
        [
            pltpu.VMEM((3, chans, 3 * LANES), BF16),
            pltpu.VMEM((2, cols + 1, n_ha, frames * rows, 3 * LANES), F32),
            dma((copies,)),
        ],
    )(slab, *settled(whole + early))
    act = lax.all_to_all(act, "ha", 0, 0)

    bias = lax.dynamic_slice_in_dim(conv_bias, ha * LANES, LANES).reshape(1, LANES)
    hbm = pl.BlockSpec(memory_space=pltpu.HBM)
    w_conv = (9, chans, 3 * LANES)
    slope, w_conv = call(
        fwd_kernel,
        (jax.ShapeDtypeStruct((cols, n_ha, frames * rows, LANES), F32), pltpu.HBM(w_conv, BF16)),
        [vmem, vmem] + [anywhere] * len(whole + early + late),
        [
            pltpu.VMEM((3, cols + 2, n_ha, frames * rows, chans), BF16),
            pltpu.VMEM(w_conv, BF16),
            dma((2 * copies,)),
            dma,
        ],
        pl.CostEstimate(flops=3 * 9 * 2 * points * LANES * chans, bytes_accessed=5 << 20, transcendentals=0),
        (vmem, hbm),
    )(slab, bias, *settled(whole + early), *settled(late))
    w_conv = in_hbm(w_conv)
    deep, high = frames * rows, 2 * rows
    shapes = [(cols, n_ha, deep), (cols, n_ha, high), (n_ha, deep), (n_ha, deep)]
    grad, head, first, last = call(
        gate_kernel, [jax.ShapeDtypeStruct((*sh, LANES), BF16) for sh in shapes], [vmem, vmem], []
    )(slope, act)

    later = shifted(head, "ta", -1)
    g_left = shifted(jnp.concatenate([last, later[cols - 1]], axis=1), "wa", 1)
    g_right = shifted(jnp.concatenate([first, later[0]], axis=1), "wa", -1)

    out = call(
        bwd_kernel,
        jax.ShapeDtypeStruct((n_ha, cols, frames * rows, chans), BF16),
        [vmem, vmem, vmem, vmem, hbm],
        [pltpu.VMEM((3, cols + 2, n_ha, frames * rows, 3 * LANES), BF16), pltpu.VMEM(w_conv.shape, BF16), dma((3,))],
    )(grad, later, g_left, g_right, w_conv)
    out = lax.all_to_all(out, "ha", 0, 0)
    out = out.astype(F32).sum(axis=0).reshape(cols, frames, rows, chans)
    return out.transpose(1, 2, 0, 3).astype(BF16)


def solution(mesh):
    in_specs = (
        P("ta", "ha", "wa", None),
        P("ta", "ha", "wa", None),
        P(),
        P(None, None, None, ("ha", "wa"), None),
        P(None, None, ("ha", "wa"), None),
    )
    return jax.shard_map(
        on_device, mesh=mesh, in_specs=in_specs, out_specs=P("ta", "ha", "wa", None), check_vma=False
    )
```

```python
import functools

import jax
import jax.numpy as jnp
from jax import lax
from jax.experimental import pallas as pl
from jax.experimental.pallas import tpu as pltpu
from jax.sharding import PartitionSpec as P

F32, BF16 = jnp.float32, jnp.bfloat16
LANES = 128
VMEM_LIMIT = 24 * 1024 * 1024


def roll_rows(x, shift):
    return pltpu.roll(x, shift, x.ndim - 2)


def row_in_block(shape):
    return lax.broadcasted_iota(jnp.int32, shape, len(shape) - 2) % 4


def from_above(x):
    prev = jnp.concatenate([jnp.zeros_like(x[:, :1]), x[:, :-1]], axis=1)
    n = x.shape[2]
    return jnp.where(row_in_block(x.shape) == 0, roll_rows(prev, n - 3), roll_rows(x, 1))


def from_below(x):
    later = jnp.concatenate([x[:, 1:], jnp.zeros_like(x[:, :1])], axis=1)
    n = x.shape[2]
    return jnp.where(row_in_block(x.shape) == 3, roll_rows(later, 3), roll_rows(x, n - 1))


def weight_copies(whole, refs, lo, first, groups, to, w_ref, sem, base=0):
    core = lax.rem(lax.axis_index("ta"), 2)
    wa = lax.axis_index("wa")
    way = 1 - 2 * core
    rounds = len(refs) // 2 + 1
    n_wa, (n_ha, _, shard, _) = 2 * rounds, whole[0].shape
    half = n_ha // 2
    copies = []

    def copy(ref, at, begin, ha, place):
        row = pl.multiple_of((ha * n_wa + place) * shard, shard)
        copies.append(
            pltpu.make_async_copy(
                ref.at[at, pl.ds(begin, groups)],
                w_ref.at[pl.ds(to, groups), pl.ds(row, shard)],
                sem.at[base + len(copies)],
            )
        )

    def behind(r):
        return lax.rem(wa + n_wa + way * r, n_wa)

    for at in range(n_ha):
        copy(whole[0], at, first, at, wa)
        copy(whole[1], at, first, at, behind(1))
        copy(whole[2], at, first, at, behind(-1))
        for r in range(2, rounds):
            copy(refs[r - 2], at, first - lo, at, behind(r))
            copy(refs[rounds - 1 + r - 2], at, first - lo, at, behind(-r))
    for at in range(half):
        copy(refs[rounds - 2], at, first - lo, core * half + at, behind(rounds))
        copy(refs[-1], at, first - lo, (1 - core) * half + at, behind(rounds))
    for one in copies:
        one.start()

    def wait():
        for one in copies:
            one.wait()

    return wait


def pack_kernel(conv_ref, up_ref, out_ref):
    for x in range(out_ref.shape[0]):
        lanes = slice(x * LANES, (x + 1) * LANES)
        for a in range(3):
            to = slice(a * LANES, (a + 1) * LANES)
            for b in range(3):
                for k in range(3):
                    out_ref[x, 3 * k + b, :, to] = conv_ref[k, a, b, :, lanes]
                out_ref[x, 9 + b, :, to] = up_ref[a, b, :, lanes]


def slab_kernel(lat_ref, past_ref, cot_ref, left_ref, right_ref, out_ref):
    n_ha, chans = out_ref.shape[0], out_ref.shape[2]
    rows, split = lat_ref.shape[1], lat_ref.shape[0] * lat_ref.shape[1]
    lat = lat_ref[...].astype(F32).reshape(split, lat_ref.shape[2], chans)
    lat = jnp.concatenate(
        [left_ref[:split].astype(F32)[None], jnp.swapaxes(lat, 0, 1), right_ref[:split].astype(F32)[None]], axis=0
    )
    first = jnp.concatenate([lat[:, :rows]] * 2, axis=1)
    past = jnp.where(lax.axis_index("ta") == 0, first, past_ref[...].astype(F32))
    lat = jnp.concatenate([past, lat], axis=1).reshape(-1, chans).astype(BF16)
    for x in range(n_ha):
        out_ref[x, : lat.shape[0]] = lat
    cot = cot_ref[...].astype(F32)
    frames, fine, cols, _ = cot.shape
    points = frames * fine // 2
    cot = cot.reshape(points, 2, cols, chans)
    for odd_row in range(2):
        part = jnp.swapaxes(cot[:, odd_row], 0, 1).astype(BF16)
        edge = slice(split + odd_row * points, split + (odd_row + 1) * points)
        columns = [left_ref[edge], *[part[w] for w in range(cols)], right_ref[edge]]
        for f, column in enumerate(columns):
            rows = pl.ds(lat.shape[0] + f // 2 * points, points)
            to = (f % 2 * 2 + odd_row) * LANES
            for x in range(n_ha):
                out_ref[x, rows, to : to + LANES] = column[:, x * LANES : (x + 1) * LANES]


def up_kernel(slab_ref, *refs):
    *blocks, out_ref, w_ref, rows_ref, sem = refs
    wait = weight_copies(blocks[:3], blocks[3:], 6, 9, 3, 0, w_ref, sem)
    n_ha = slab_ref.shape[0]
    for par in range(2):
        cot = jnp.stack([slab_ref[x, 240:384, :] for x in range(n_ha)], axis=0)
        cot = cot[:, :, 2 * par * LANES : 2 * (par + 1) * LANES].astype(F32)
        cot = jnp.stack([cot[x].reshape(9, 16, 2 * LANES) for x in range(n_ha)], axis=1)
        even, odd = cot[..., :LANES], cot[..., LANES:]
        rows_ref[par, :, :, :, 0:LANES] = odd + from_below(even)
        rows_ref[par, :, :, :, LANES : 2 * LANES] = even + odd
        rows_ref[par, :, :, :, 2 * LANES : 3 * LANES] = even + from_above(odd)
    wait()
    total = None
    for b in range(3):
        box = None
        for e in (1 - b, 2 - b):
            par, off = (e + 1) % 2, (e + 1) // 2
            part = rows_ref[par, off : off + 8]
            box = part if box is None else box + part
        box = box.reshape(-1, 3 * LANES)
        high = box.astype(BF16)
        low = (box - high.astype(F32)).astype(BF16)
        term = lax.dot_general(
            jnp.concatenate([high, low], axis=1),
            jnp.concatenate([w_ref[b], w_ref[b]], axis=1),
            (((1,), (1,)), ((), ())),
            preferred_element_type=F32,
        )
        total = term if total is None else total + term
    for x in range(n_ha):
        out_ref[x] = total[:, x * LANES : (x + 1) * LANES].astype(BF16)


def fwd_kernel(slab_ref, bias_ref, *refs):
    *blocks, out_ref, w_hbm, win_ref, w_ref, sem, out_sem = refs
    whole, early, late = blocks[:3], blocks[3 : 3 + (len(blocks) - 3) // 2], blocks[3 + (len(blocks) - 3) // 2 :]
    early_wait = weight_copies(whole, early, 6, 6, 3, 6, w_ref, sem)
    late_wait = weight_copies(whole, late, 0, 0, 6, 0, w_ref, sem, sem.shape[0] // 2)
    n_ha = slab_ref.shape[0]
    for x in range(n_ha):
        for pair in range(5):
            two = slab_ref[x, pair * 48 : pair * 48 + 48, :].astype(F32)
            for one in range(2):
                for k in range(3):
                    lo = one * 24 + 4 * k
                    win_ref[k, 2 * pair + one, x] = two[lo : lo + 16].astype(BF16)
    early_wait()
    total = None
    for k in (2, 0, 1):
        if k == 0:
            late_wait()
            keep = pltpu.make_async_copy(w_ref, w_hbm, out_sem)
            keep.start()
        for b in range(3):
            window = win_ref[k, b : b + 8].reshape(-1, win_ref.shape[-1])
            term = jnp.dot(window, w_ref[3 * k + b], preferred_element_type=F32)
            total = term if total is None else total + term
    total = total.reshape(8, n_ha, 16, 3 * LANES)
    pre = (
        from_above(total[..., :LANES])
        + total[..., LANES : 2 * LANES]
        + from_below(total[..., 2 * LANES :])
        + bias_ref[...].reshape(1, 1, 1, LANES)
    )
    sig = 1.0 / (1.0 + jnp.exp(-pre))
    out_ref[...] = sig * (1.0 + pre * (1.0 - sig))
    keep.wait()


def gate_kernel(slope_ref, act_ref, out_ref, head_ref, first_ref, last_ref):
    grad = act_ref[0].astype(F32)
    for x in range(1, act_ref.shape[0]):
        grad = grad + act_ref[x].astype(F32)
    grad = (grad.reshape(slope_ref.shape) * slope_ref[...]).astype(BF16)
    out_ref[...] = grad
    first_ref[...] = grad[0]
    last_ref[...] = grad[-1]
    head_ref[...] = grad[:, :, : head_ref.shape[2]]


def bwd_kernel(g_ref, later_ref, left_ref, right_ref, w_hbm, out_ref, win_ref, w_ref, sem):
    fetch = [
        pltpu.make_async_copy(w_hbm.at[pl.ds(3 * k, 3)], w_ref.at[pl.ds(3 * k, 3)], sem.at[k]) for k in range(3)
    ]
    for copy in fetch:
        copy.start()
    n_ha = g_ref.shape[1]
    at_start = (lax.axis_index("ta") == 0).astype(F32)
    grad = jnp.concatenate([g_ref[...].astype(F32), later_ref[...].astype(F32)], axis=2)
    grad = jnp.concatenate(
        [left_ref[...].astype(F32)[None], grad, right_ref[...].astype(F32)[None]], axis=0
    )
    zero, one, two = grad[:, :, 0:4], grad[:, :, 4:8], grad[:, :, 8:12]
    windows = [
        grad[:, :, 0:16],
        jnp.concatenate([one + at_start * zero, grad[:, :, 8:20]], axis=2),
        jnp.concatenate([two + at_start * (zero + one), grad[:, :, 12:24]], axis=2),
    ]
    for shift in range(3):
        x = windows[shift]
        win_ref[shift, :, :, :, 0:LANES] = from_below(x).astype(BF16)
        win_ref[shift, :, :, :, LANES : 2 * LANES] = x.astype(BF16)
        win_ref[shift, :, :, :, 2 * LANES : 3 * LANES] = from_above(x).astype(BF16)
    total = None
    taps = [(k, b) for k in range(3) for b in range(3)]
    for few in (taps[0:2], taps[2:4], taps[4:6], taps[6:8], taps[8:9]):
        for k, b in few:
            if b == 0:
                fetch[k].wait()
        term = lax.dot_general(
            jnp.concatenate([win_ref[2 - k, 2 - b : 10 - b].reshape(-1, 3 * LANES) for k, b in few], axis=1),
            jnp.concatenate([w_ref[3 * k + b] for k, b in few], axis=1),
            (((1,), (1,)), ((), ())),
            preferred_element_type=F32,
        )
        total = term if total is None else total + term
    total = total.astype(BF16).reshape(8, n_ha, 16, -1)
    for x in range(n_ha):
        out_ref[x] = total[:, x]


def call(kernel, out_shape, specs, scratch, cost=None, outs=None):
    return pl.pallas_call(
        kernel,
        out_shape=out_shape,
        in_specs=specs,
        out_specs=outs or jax.tree.map(lambda _: pl.BlockSpec(memory_space=pltpu.VMEM), out_shape),
        scratch_shapes=scratch,
        cost_estimate=cost,
        compiler_params=pltpu.CompilerParams(vmem_limit_bytes=VMEM_LIMIT),
    )


def in_hbm(x):
    return pltpu.with_memory_space_constraint(x, pltpu.HBM)


def settled(blocks):
    return [x if x.shape[0] == 2 else in_hbm(x) for x in blocks]


def shifted(x, axis, step):
    n = lax.axis_size(axis)
    return lax.ppermute(x, axis, [(i, i + step) for i in range(n) if 0 <= i + step < n])


def on_device(latent, cotangent, conv_bias, conv_weight, up_weight):
    frames, rows, cols, chans = latent.shape
    n_ta, n_ha, n_wa = (lax.axis_size(a) for a in ("ta", "ha", "wa"))
    ta, ha = lax.axis_index("ta"), lax.axis_index("ha")
    shard = conv_weight.shape[3]
    core = lax.rem(ta, 2)

    vmem, anywhere = pl.BlockSpec(memory_space=pltpu.VMEM), pl.BlockSpec(memory_space=pl.ANY)
    groups = call(
        pack_kernel,
        jax.ShapeDtypeStruct((n_ha, 12, shard, 3 * LANES), BF16),
        [vmem, vmem],
        [],
    )(in_hbm(conv_weight), in_hbm(up_weight))
    def edge(col_l, col_c):
        fine = cotangent[:, :, col_c].reshape(frames * rows, 2, chans).transpose(1, 0, 2)
        return jnp.concatenate([latent[:, :, col_l].reshape(-1, chans), fine.reshape(-1, chans)], axis=0)

    left = shifted(edge(cols - 1, 2 * cols - 1), "wa", 1)
    right = shifted(edge(0, 0), "wa", -1)
    tail = slice((frames - 2) * rows, frames * rows)
    middle = latent[frames - 2 :].transpose(2, 0, 1, 3).reshape(cols, 2 * rows, chans)
    past = shifted(jnp.concatenate([left[None, tail], middle, right[None, tail]], axis=0), "ta", 1)
    groups = lax.all_to_all(groups, "ha", 0, 0)
    length = (cols + 2) * (frames + 2) * rows + (cols + 1) * frames * rows
    slab = call(
        slab_kernel, jax.ShapeDtypeStruct((n_ha, length, chans), BF16), [vmem] * 5, []
    )(latent, past, cotangent, left, right)

    swap = [(i, i ^ 1) for i in range(n_ta)]
    around = [
        (t * n_wa + (w + 1 - 2 * (t % 2)) % n_wa, t * n_wa + w) for t in range(n_ta) for w in range(n_wa)
    ]
    spans = [(6, 12), (0, 6)]
    block = lax.ppermute(groups, ("ta", "wa"), around)
    swapped = lax.ppermute(block, "ta", swap)
    mine, others = [], []
    for lo, hi in spans:
        mine.append([block[:, lo:hi]])
        others.append([])
    for r in range(2, n_wa // 2):
        for q in range(2):
            mine[q].append(lax.ppermute(mine[q][-1], ("ta", "wa"), around))
            others[q].append(lax.ppermute(mine[q][-1], "ta", swap))
    halves = [lax.dynamic_slice_in_dim(m[-1], core * (n_ha // 2), n_ha // 2, axis=0) for m in mine]
    lasts = [lax.ppermute(x, ("ta", "wa"), around) for x in halves]
    lasts[0], _ = lax.optimization_barrier((lasts[0], halves[1]))
    for q in range(2):
        mine[q].append(lasts[q])
        others[q].append(lax.ppermute(lasts[q], "ta", swap))
    whole = [groups, block, swapped]
    slab = lax.all_to_all(slab, "ha", 0, 0)
    early, late = mine[0][1:] + others[0], mine[1][1:] + others[1]

    points = cols * n_ha * frames * rows
    copies = (n_wa - 1) * n_ha + n_ha
    dma = pltpu.SemaphoreType.DMA
    act = call(
        up_kernel,
        jax.ShapeDtypeStruct((n_ha, points, LANES), BF16),
        [vmem] + [anywhere] * len(whole + early),
        [
            pltpu.VMEM((3, chans, 3 * LANES), BF16),
            pltpu.VMEM((2, cols + 1, n_ha, frames * rows, 3 * LANES), F32),
            dma((copies,)),
        ],
    )(slab, *settled(whole + early))
    act = lax.all_to_all(act, "ha", 0, 0)

    bias = lax.dynamic_slice_in_dim(conv_bias, ha * LANES, LANES).reshape(1, LANES)
    hbm = pl.BlockSpec(memory_space=pltpu.HBM)
    w_conv = (9, chans, 3 * LANES)
    slope, w_conv = call(
        fwd_kernel,
        (jax.ShapeDtypeStruct((cols, n_ha, frames * rows, LANES), F32), pltpu.HBM(w_conv, BF16)),
        [vmem, vmem] + [anywhere] * len(whole + early + late),
        [
            pltpu.VMEM((3, cols + 2, n_ha, frames * rows, chans), BF16),
            pltpu.VMEM(w_conv, BF16),
            dma((2 * copies,)),
            dma,
        ],
        pl.CostEstimate(flops=3 * 9 * 2 * points * LANES * chans, bytes_accessed=5 << 20, transcendentals=0),
        (vmem, hbm),
    )(slab, bias, *settled(whole + early), *settled(late))
    w_conv = in_hbm(w_conv)
    deep, high = frames * rows, 2 * rows
    shapes = [(cols, n_ha, deep), (cols, n_ha, high), (n_ha, deep), (n_ha, deep)]
    grad, head, first, last = call(
        gate_kernel, [jax.ShapeDtypeStruct((*sh, LANES), BF16) for sh in shapes], [vmem, vmem], []
    )(slope, act)

    later = shifted(head, "ta", -1)
    g_left = shifted(jnp.concatenate([last, later[cols - 1]], axis=1), "wa", 1)
    g_right = shifted(jnp.concatenate([first, later[0]], axis=1), "wa", -1)

    out = call(
        bwd_kernel,
        jax.ShapeDtypeStruct((n_ha, cols, frames * rows, chans), BF16),
        [vmem, vmem, vmem, vmem, hbm],
        [pltpu.VMEM((3, cols + 2, n_ha, frames * rows, 3 * LANES), BF16), pltpu.VMEM(w_conv.shape, BF16), dma((3,))],
    )(grad, later, g_left, g_right, w_conv)
    out = lax.all_to_all(out, "ha", 0, 0)
    out = out.astype(F32).sum(axis=0).reshape(cols, frames, rows, chans)
    return out.transpose(1, 2, 0, 3).astype(BF16)


def solution(mesh):
    in_specs = (
        P("ta", "ha", "wa", None),
        P("ta", "ha", "wa", None),
        P(),
        P(None, None, None, ("ha", "wa"), None),
        P(None, None, ("ha", "wa"), None),
    )
    return jax.shard_map(
        on_device, mesh=mesh, in_specs=in_specs, out_specs=P("ta", "ha", "wa", None), check_vma=False
    )
```

```python
import functools

import jax
import jax.numpy as jnp
from jax import lax
from jax.experimental import pallas as pl
from jax.experimental.pallas import tpu as pltpu
from jax.sharding import PartitionSpec as P

F32, BF16 = jnp.float32, jnp.bfloat16
LANES = 128
VMEM_LIMIT = 24 * 1024 * 1024


def roll_rows(x, shift):
    return pltpu.roll(x, shift, x.ndim - 2)


def row_in_block(shape):
    return lax.broadcasted_iota(jnp.int32, shape, len(shape) - 2) % 4


def from_above(x):
    prev = jnp.concatenate([jnp.zeros_like(x[:, :1]), x[:, :-1]], axis=1)
    n = x.shape[2]
    return jnp.where(row_in_block(x.shape) == 0, roll_rows(prev, n - 3), roll_rows(x, 1))


def from_below(x):
    later = jnp.concatenate([x[:, 1:], jnp.zeros_like(x[:, :1])], axis=1)
    n = x.shape[2]
    return jnp.where(row_in_block(x.shape) == 3, roll_rows(later, 3), roll_rows(x, n - 1))


def weight_copies(whole, refs, lo, first, groups, to, w_ref, sem, base=0, stages=(0, 1)):
    core = lax.rem(lax.axis_index("ta"), 2)
    wa = lax.axis_index("wa")
    way = 1 - 2 * core
    rounds = len(refs) // 2 + 1
    n_wa, (n_ha, _, shard, _) = 2 * rounds, whole[0].shape
    half = n_ha // 2
    copies = []

    def copy(ref, at, begin, ha, place):
        row = pl.multiple_of((ha * n_wa + place) * shard, shard)
        copies.append(
            pltpu.make_async_copy(
                ref.at[at, pl.ds(begin, groups)],
                w_ref.at[pl.ds(to, groups), pl.ds(row, shard)],
                sem.at[base + len(copies)],
            )
        )

    def behind(r):
        return lax.rem(wa + n_wa + way * r, n_wa)

    for at in range(n_ha if 0 in stages else 0):
        copy(whole[0], at, first, at, wa)
        copy(whole[1], at, first, at, behind(1))
        copy(whole[2], at, first, at, behind(-1))
        for r in range(2, rounds):
            copy(refs[r - 2], at, first - lo, at, behind(r))
            copy(refs[rounds - 1 + r - 2], at, first - lo, at, behind(-r))
    for at in range(half if 1 in stages else 0):
        copy(refs[rounds - 2], at, first - lo, core * half + at, behind(rounds))
        copy(refs[-1], at, first - lo, (1 - core) * half + at, behind(rounds))
    for one in copies:
        one.start()

    def wait():
        for one in copies:
            one.wait()

    return wait


def pack_kernel(conv_ref, up_ref, out_ref):
    for x in range(out_ref.shape[0]):
        lanes = slice(x * LANES, (x + 1) * LANES)
        for a in range(3):
            to = slice(a * LANES, (a + 1) * LANES)
            for b in range(3):
                for k in range(3):
                    out_ref[x, 3 * k + b, :, to] = conv_ref[k, a, b, :, lanes]
                out_ref[x, 9 + b, :, to] = up_ref[a, b, :, lanes]


def slab_kernel(lat_ref, past_ref, cot_ref, left_ref, right_ref, out_ref):
    n_ha, chans = out_ref.shape[0], out_ref.shape[2]
    rows, split = lat_ref.shape[1], lat_ref.shape[0] * lat_ref.shape[1]
    lat = lat_ref[...].astype(F32).reshape(split, lat_ref.shape[2], chans)
    lat = jnp.concatenate(
        [left_ref[:split].astype(F32)[None], jnp.swapaxes(lat, 0, 1), right_ref[:split].astype(F32)[None]], axis=0
    )
    first = jnp.concatenate([lat[:, :rows]] * 2, axis=1)
    past = jnp.where(lax.axis_index("ta") == 0, first, past_ref[...].astype(F32))
    lat = jnp.concatenate([past, lat], axis=1).reshape(-1, chans).astype(BF16)
    for x in range(n_ha):
        out_ref[x, : lat.shape[0]] = lat
    cot = cot_ref[...].astype(F32)
    frames, fine, cols, _ = cot.shape
    points = frames * fine // 2
    cot = cot.reshape(points, 2, cols, chans)
    for odd_row in range(2):
        part = jnp.swapaxes(cot[:, odd_row], 0, 1).astype(BF16)
        edge = slice(split + odd_row * points, split + (odd_row + 1) * points)
        columns = [left_ref[edge], *[part[w] for w in range(cols)], right_ref[edge]]
        for f, column in enumerate(columns):
            rows = pl.ds(lat.shape[0] + f // 2 * points, points)
            to = (f % 2 * 2 + odd_row) * LANES
            for x in range(n_ha):
                out_ref[x, rows, to : to + LANES] = column[:, x * LANES : (x + 1) * LANES]


def up_early_kernel(*refs):
    *blocks, out_ref, sem = refs
    mine, others = blocks[3 : 3 + (len(blocks) - 3) // 2], blocks[3 + (len(blocks) - 3) // 2 :]
    weight_copies(blocks[:3], [*mine, None, *others, None], 6, 9, 3, 0, out_ref, sem, stages=(0,))()


def box_kernel(slab_ref, out_ref, rows_ref):
    n_ha = slab_ref.shape[0]
    for par in range(2):
        cot = jnp.stack([slab_ref[x, 240:384, :] for x in range(n_ha)], axis=0)
        cot = cot[:, :, 2 * par * LANES : 2 * (par + 1) * LANES].astype(F32)
        cot = jnp.stack([cot[x].reshape(9, 16, 2 * LANES) for x in range(n_ha)], axis=1)
        even, odd = cot[..., :LANES], cot[..., LANES:]
        rows_ref[par, :, :, :, 0:LANES] = odd + from_below(even)
        rows_ref[par, :, :, :, LANES : 2 * LANES] = even + odd
        rows_ref[par, :, :, :, 2 * LANES : 3 * LANES] = even + from_above(odd)
    for b in range(3):
        box = None
        for e in (1 - b, 2 - b):
            par, off = (e + 1) % 2, (e + 1) // 2
            part = rows_ref[par, off : off + 8]
            box = part if box is None else box + part
        box = box.reshape(-1, 3 * LANES)
        high = box.astype(BF16)
        out_ref[b, :, : 3 * LANES] = high
        out_ref[b, :, 3 * LANES :] = (box - high.astype(F32)).astype(BF16)


def up_kernel(box_ref, early_ref, *refs):
    *blocks, out_ref, w_ref, sem = refs
    w_ref[...] = early_ref[...]
    wait = weight_copies(blocks[:3], blocks[3:], 6, 9, 3, 0, w_ref, sem, stages=(1,))
    wait()
    total = None
    for b in range(3):
        term = lax.dot_general(
            box_ref[b],
            jnp.concatenate([w_ref[b], w_ref[b]], axis=1),
            (((1,), (1,)), ((), ())),
            preferred_element_type=F32,
        )
        total = term if total is None else total + term
    for x in range(out_ref.shape[0]):
        out_ref[x] = total[:, x * LANES : (x + 1) * LANES].astype(BF16)


def fwd_kernel(slab_ref, bias_ref, *refs):
    *blocks, out_ref, w_hbm, win_ref, w_ref, sem, out_sem = refs
    whole, early, late = blocks[:3], blocks[3 : 3 + (len(blocks) - 3) // 2], blocks[3 + (len(blocks) - 3) // 2 :]
    early_wait = weight_copies(whole, early, 6, 6, 3, 6, w_ref, sem)
    late_wait = weight_copies(whole, late, 0, 0, 6, 0, w_ref, sem, sem.shape[0] // 2)
    n_ha = slab_ref.shape[0]
    for x in range(n_ha):
        for pair in range(5):
            two = slab_ref[x, pair * 48 : pair * 48 + 48, :].astype(F32)
            for one in range(2):
                for k in range(3):
                    lo = one * 24 + 4 * k
                    win_ref[k, 2 * pair + one, x] = two[lo : lo + 16].astype(BF16)
    early_wait()
    total = None
    for k in (2, 0, 1):
        if k == 0:
            late_wait()
            keep = pltpu.make_async_copy(w_ref, w_hbm, out_sem)
            keep.start()
        for b in range(3):
            window = win_ref[k, b : b + 8].reshape(-1, win_ref.shape[-1])
            term = jnp.dot(window, w_ref[3 * k + b], preferred_element_type=F32)
            total = term if total is None else total + term
    total = total.reshape(8, n_ha, 16, 3 * LANES)
    pre = (
        from_above(total[..., :LANES])
        + total[..., LANES : 2 * LANES]
        + from_below(total[..., 2 * LANES :])
        + bias_ref[...].reshape(1, 1, 1, LANES)
    )
    sig = 1.0 / (1.0 + jnp.exp(-pre))
    out_ref[...] = sig * (1.0 + pre * (1.0 - sig))
    keep.wait()


def gate_kernel(slope_ref, act_ref, out_ref, head_ref, first_ref, last_ref):
    grad = act_ref[0].astype(F32)
    for x in range(1, act_ref.shape[0]):
        grad = grad + act_ref[x].astype(F32)
    grad = (grad.reshape(slope_ref.shape) * slope_ref[...]).astype(BF16)
    out_ref[...] = grad
    first_ref[...] = grad[0]
    last_ref[...] = grad[-1]
    head_ref[...] = grad[:, :, : head_ref.shape[2]]


def bwd_kernel(g_ref, later_ref, left_ref, right_ref, w_hbm, out_ref, win_ref, w_ref, sem):
    fetch = [
        pltpu.make_async_copy(w_hbm.at[pl.ds(3 * k, 3)], w_ref.at[pl.ds(3 * k, 3)], sem.at[k]) for k in range(3)
    ]
    for copy in fetch:
        copy.start()
    n_ha = g_ref.shape[1]
    at_start = (lax.axis_index("ta") == 0).astype(F32)
    grad = jnp.concatenate([g_ref[...].astype(F32), later_ref[...].astype(F32)], axis=2)
    grad = jnp.concatenate(
        [left_ref[...].astype(F32)[None], grad, right_ref[...].astype(F32)[None]], axis=0
    )
    shifted_rows = (from_below(grad), grad, from_above(grad))
    for a, x in enumerate(shifted_rows):
        zero, one, two = x[:, :, 0:4], x[:, :, 4:8], x[:, :, 8:12]
        windows = (
            x[:, :, 0:16],
            jnp.concatenate([one + at_start * zero, x[:, :, 8:20]], axis=2),
            jnp.concatenate([two + at_start * (zero + one), x[:, :, 12:24]], axis=2),
        )
        for shift, window in enumerate(windows):
            win_ref[shift, :, :, :, a * LANES : (a + 1) * LANES] = window.astype(BF16)
    total = None
    taps = [(k, b) for k in range(3) for b in range(3)]
    for few in (taps[0:2], taps[2:4], taps[4:6], taps[6:8], taps[8:9]):
        for k, b in few:
            if b == 0:
                fetch[k].wait()
        term = lax.dot_general(
            jnp.concatenate([win_ref[2 - k, 2 - b : 10 - b].reshape(-1, 3 * LANES) for k, b in few], axis=1),
            jnp.concatenate([w_ref[3 * k + b] for k, b in few], axis=1),
            (((1,), (1,)), ((), ())),
            preferred_element_type=F32,
        )
        total = term if total is None else total + term
    total = total.astype(BF16).reshape(8, n_ha, 16, -1)
    for x in range(n_ha):
        out_ref[x] = total[:, x]


def call(kernel, out_shape, specs, scratch, cost=None, outs=None):
    return pl.pallas_call(
        kernel,
        out_shape=out_shape,
        in_specs=specs,
        out_specs=outs or jax.tree.map(lambda _: pl.BlockSpec(memory_space=pltpu.VMEM), out_shape),
        scratch_shapes=scratch,
        cost_estimate=cost,
        compiler_params=pltpu.CompilerParams(vmem_limit_bytes=VMEM_LIMIT),
    )


def in_hbm(x):
    return pltpu.with_memory_space_constraint(x, pltpu.HBM)


def settled(blocks):
    return [x if x.shape[0] == 2 else in_hbm(x) for x in blocks]


def shifted(x, axis, step):
    n = lax.axis_size(axis)
    return lax.ppermute(x, axis, [(i, i + step) for i in range(n) if 0 <= i + step < n])


def on_device(latent, cotangent, conv_bias, conv_weight, up_weight):
    frames, rows, cols, chans = latent.shape
    n_ta, n_ha, n_wa = (lax.axis_size(a) for a in ("ta", "ha", "wa"))
    ta, ha = lax.axis_index("ta"), lax.axis_index("ha")
    shard = conv_weight.shape[3]
    core = lax.rem(ta, 2)

    vmem, anywhere = pl.BlockSpec(memory_space=pltpu.VMEM), pl.BlockSpec(memory_space=pl.ANY)
    groups = call(
        pack_kernel,
        jax.ShapeDtypeStruct((n_ha, 12, shard, 3 * LANES), BF16),
        [vmem, vmem],
        [],
    )(in_hbm(conv_weight), in_hbm(up_weight))
    def edge(col_l, col_c):
        fine = cotangent[:, :, col_c].reshape(frames * rows, 2, chans).transpose(1, 0, 2)
        return jnp.concatenate([latent[:, :, col_l].reshape(-1, chans), fine.reshape(-1, chans)], axis=0)

    left = shifted(edge(cols - 1, 2 * cols - 1), "wa", 1)
    right = shifted(edge(0, 0), "wa", -1)
    tail = slice((frames - 2) * rows, frames * rows)
    middle = latent[frames - 2 :].transpose(2, 0, 1, 3).reshape(cols, 2 * rows, chans)
    past = shifted(jnp.concatenate([left[None, tail], middle, right[None, tail]], axis=0), "ta", 1)
    groups = lax.all_to_all(groups, "ha", 0, 0)
    length = (cols + 2) * (frames + 2) * rows + (cols + 1) * frames * rows
    slab = call(
        slab_kernel, jax.ShapeDtypeStruct((n_ha, length, chans), BF16), [vmem] * 5, []
    )(latent, past, cotangent, left, right)

    swap = [(i, i ^ 1) for i in range(n_ta)]
    around = [
        (t * n_wa + (w + 1 - 2 * (t % 2)) % n_wa, t * n_wa + w) for t in range(n_ta) for w in range(n_wa)
    ]
    spans = [(6, 12), (0, 6)]
    block = lax.ppermute(groups, ("ta", "wa"), around)
    swapped = lax.ppermute(block, "ta", swap)
    mine, others = [], []
    for lo, hi in spans:
        mine.append([block[:, lo:hi]])
        others.append([])
    for r in range(2, n_wa // 2):
        for q in range(2):
            mine[q].append(lax.ppermute(mine[q][-1], ("ta", "wa"), around))
            others[q].append(lax.ppermute(mine[q][-1], "ta", swap))
    halves = [lax.dynamic_slice_in_dim(m[-1], core * (n_ha // 2), n_ha // 2, axis=0) for m in mine]
    lasts = [lax.ppermute(x, ("ta", "wa"), around) for x in halves]
    before = [groups, block, swapped, *mine[0][1:], *others[0]]
    up_early = call(
        up_early_kernel,
        jax.ShapeDtypeStruct((3, chans, 3 * LANES), BF16),
        [anywhere] * len(before),
        [pltpu.SemaphoreType.DMA((n_wa * n_ha,))],
    )(*map(in_hbm, before))
    slab = lax.all_to_all(slab, "ha", 0, 0)
    points = cols * n_ha * frames * rows
    boxes = call(
        box_kernel,
        jax.ShapeDtypeStruct((3, points, 6 * LANES), BF16),
        [vmem],
        [pltpu.VMEM((2, cols + 1, n_ha, frames * rows, 3 * LANES), F32)],
    )(slab)
    lasts[0], up_early, boxes, _ = lax.optimization_barrier((lasts[0], up_early, boxes, halves[1]))
    for q in range(2):
        mine[q].append(lasts[q])
        others[q].append(lax.ppermute(lasts[q], "ta", swap))
    whole = [groups, block, swapped]
    early, late = mine[0][1:] + others[0], mine[1][1:] + others[1]

    points = cols * n_ha * frames * rows
    copies = (n_wa - 1) * n_ha + n_ha
    dma = pltpu.SemaphoreType.DMA
    act = call(
        up_kernel,
        jax.ShapeDtypeStruct((n_ha, points, LANES), BF16),
        [vmem, vmem] + [anywhere] * len(whole + early),
        [
            pltpu.VMEM((3, chans, 3 * LANES), BF16),
            dma((copies,)),
        ],
    )(boxes, up_early, *settled(whole + early))
    act = lax.all_to_all(act, "ha", 0, 0)

    bias = lax.dynamic_slice_in_dim(conv_bias, ha * LANES, LANES).reshape(1, LANES)
    hbm = pl.BlockSpec(memory_space=pltpu.HBM)
    w_conv = (9, chans, 3 * LANES)
    slope, w_conv = call(
        fwd_kernel,
        (jax.ShapeDtypeStruct((cols, n_ha, frames * rows, LANES), F32), pltpu.HBM(w_conv, BF16)),
        [vmem, vmem] + [anywhere] * len(whole + early + late),
        [
            pltpu.VMEM((3, cols + 2, n_ha, frames * rows, chans), BF16),
            pltpu.VMEM(w_conv, BF16),
            dma((2 * copies,)),
            dma,
        ],
        pl.CostEstimate(flops=3 * 9 * 2 * points * LANES * chans, bytes_accessed=5 << 20, transcendentals=0),
        (vmem, hbm),
    )(slab, bias, *settled(whole + early), *settled(late))
    w_conv = in_hbm(w_conv)
    deep, high = frames * rows, 2 * rows
    shapes = [(cols, n_ha, deep), (cols, n_ha, high), (n_ha, deep), (n_ha, deep)]
    grad, head, first, last = call(
        gate_kernel, [jax.ShapeDtypeStruct((*sh, LANES), BF16) for sh in shapes], [vmem, vmem], []
    )(slope, act)

    later = shifted(head, "ta", -1)
    g_left = shifted(jnp.concatenate([last, later[cols - 1]], axis=1), "wa", 1)
    g_right = shifted(jnp.concatenate([first, later[0]], axis=1), "wa", -1)

    out = call(
        bwd_kernel,
        jax.ShapeDtypeStruct((n_ha, cols, frames * rows, chans), BF16),
        [vmem, vmem, vmem, vmem, hbm],
        [pltpu.VMEM((3, cols + 2, n_ha, frames * rows, 3 * LANES), BF16), pltpu.VMEM(w_conv.shape, BF16), dma((3,))],
    )(grad, later, g_left, g_right, w_conv)
    out = lax.all_to_all(out, "ha", 0, 0)
    out = out.astype(F32).sum(axis=0).reshape(cols, frames, rows, chans)
    return out.transpose(1, 2, 0, 3).astype(BF16)


def solution(mesh):
    in_specs = (
        P("ta", "ha", "wa", None),
        P("ta", "ha", "wa", None),
        P(),
        P(None, None, None, ("ha", "wa"), None),
        P(None, None, ("ha", "wa"), None),
    )
    return jax.shard_map(
        on_device, mesh=mesh, in_specs=in_specs, out_specs=P("ta", "ha", "wa", None), check_vma=False
    )
```
